32 devices in a mesh: row: 8 (over z, x), col: 4 (over y, core).
Axes of the slice: x: 2, y: 2, z: 4, core: 2. Of those that a mesh axis runs over, the one named last changes fastest.
Arguments:
- features: bfloat16 [4096, 1024], P(('row', 'col')), may hold values from -6 to 6
- weight: bfloat16 [1024, 1024], replicated, may hold values from -0.1875 to 0.1875
- cotangent: bfloat16 [4096, 1024], P(('col', 'row')), may hold values from -6 to 6
- tile_values: bfloat16 [8, 4, 8, 128, 128], P('row', 'col'), may hold values from -0.5 to 0.5
- block_row: int32 [8, 4, 8], P('row', 'col'), may hold values from 0 to 7, as said below
- block_column: int32 [8, 4, 8], P('row', 'col'), may hold values from 0 to 3, as said below
- tile_count: int32 [8, 4], P('row', 'col'), may hold values from 2 to 8, as said below
Outputs:
- activated: bfloat16 [4096, 1024], P(('col', 'row'))
- feat_grad: bfloat16 [4096, 1024], P(('row', 'col'))
- weight_grad: float32 [1024, 1024], replicated
The draws below stay inside these ranges and needn't reach their ends.
Inputs may be any that keep to these rules, and one draw needn't show every extreme that they name: `block_row`: within one grid position the slots name distinct region cells. `block_column`: within one grid position the slots name distinct region cells. `tile_count`: some grid position has exactly 8 live slots.
All inputs are finite; a program needn't handle non-finite values.
Results may differ from the reference program's by a relative error of at most 0.02.
Values may be sent and summed in bfloat16 or wider, within the bound.
No kernel may reach another device: no remote copies, remote signals or barrier semaphores. Data moves between devices by JAX's collectives and lax.ppermute only.
A program may use at most 128 MiB of HBM per device.

```python
import jax
import jax.numpy as jnp
from jax import lax

F = 1024
BLK = 128
RB_DEV = 1
NODES = 4096
REGION_ROWS = 8
REGION_COLS = 4
TILES = 8
N_ROW = 8
N_COL = 4


def region_cells(key):
    keys = jax.random.split(jax.random.fold_in(key, 11), N_ROW * N_COL)

    def pick_cells(single):
        return jax.random.permutation(single, REGION_ROWS * REGION_COLS)[:TILES]
    cells = jax.vmap(pick_cells)(keys).astype(jnp.int32)
    return cells.reshape(N_ROW, N_COL, TILES)


def draw_block_row(key, part):
    return region_cells(key) // REGION_COLS


def draw_block_column(key, part):
    return region_cells(key) % REGION_COLS


def draw_tile_count(key, part):
    counts = jax.random.randint(jax.random.fold_in(key, 5), (N_ROW * N_COL,), TILES // 4, TILES + 1)
    chosen = jax.random.randint(jax.random.fold_in(key, 7), (), 0, N_ROW * N_COL)
    places = jnp.arange(N_ROW * N_COL, dtype=jnp.int32)
    counts = jnp.where(places == chosen, TILES, counts)
    return counts.astype(jnp.int32).reshape(N_ROW, N_COL)


def shard_levels(own_key, dims, cuts, smallest, top_value):
    def one(axis_at, shards_of):
        heights = jax.random.uniform(jax.random.fold_in(jax.random.fold_in(own_key, 6), axis_at), (shards_of,), jnp.float32, smallest / len(cuts), top_value / len(cuts))
        return jnp.repeat(jnp.exp(heights), dims[axis_at] // shards_of).reshape((-1,) + (1,) * (len(dims) - axis_at - 1))

    factor_of = one(*cuts[0])
    for cut in cuts[1:]:
        factor_of = factor_of * one(*cut)
    return factor_of


def centred(stream_key, shape, scale, most, cuts=(), held_as=jnp.bfloat16):
    gain = shard_levels(stream_key, shape, cuts, -0.22, 0.18) if cuts else 1.0
    drawn = jax.random.normal(stream_key, shape, jnp.float32) * scale * gain
    return jnp.minimum(jnp.maximum(drawn, -most), most).astype(held_as)


def setup_inputs(seed: int = 0) -> dict:
    key_list = jax.random.split(jax.random.key(seed), 8)
    features = centred(key_list[0], (NODES, F), 1.0, 6.0, ((0, 32),))
    weight = centred(key_list[1], (F, F), F ** -0.5, 0.1875)
    cotangent = centred(key_list[2], (NODES, F), 1.0, 6.0, ((0, 32),))
    tile_values = centred(key_list[3], (N_ROW, N_COL, TILES, BLK, BLK), (1.2 * (TILES * BLK // RB_DEV) ** -0.5), 0.5, ((0, 8), (1, 4)))
    block_row = draw_block_row(jax.random.fold_in(key_list[7], 71), 0)
    block_column = draw_block_column(jax.random.fold_in(key_list[7], 71), 0)
    tile_count = draw_tile_count(jax.random.fold_in(key_list[7], 71), 0)
    return dict(features=features, weight=weight, cotangent=cotangent, tile_values=tile_values, block_row=block_row, block_column=block_column, tile_count=tile_count)


def silu_slope(hidden):
    sigmoid = jax.nn.sigmoid(hidden)
    return sigmoid * (1.0 + hidden * (1.0 - sigmoid))


def spread_tiles(source, tile_block, index_in, index_out, is_live, out_blocks, flipped):
    blocks = source.reshape(-1, BLK, F).astype(jnp.float32)
    picked = blocks[index_in]
    matrix = tile_block.astype(jnp.float32)
    form = "tba,tbf->taf" if flipped else "tab,tbf->taf"
    products = jnp.einsum(form, matrix, picked, precision=lax.Precision.HIGHEST)
    products = products * is_live.astype(jnp.float32)[:, None, None]
    summed = jax.ops.segment_sum(products, index_out, num_segments=out_blocks)
    return summed.reshape(out_blocks * BLK, F)


def reference(features, weight, cotangent, tile_values, block_row, block_column, tile_count):
    span = BLK * RB_DEV
    projected = jnp.dot(features, weight, preferred_element_type=jnp.float32).astype(jnp.bfloat16)
    slots = jnp.arange(TILES, dtype=jnp.int32)

    def forward_group(column):
        def add_row(grid_row, accum):
            first = (grid_row * (N_COL * span)).astype(jnp.int32)
            source = lax.dynamic_slice_in_dim(projected, first, N_COL * span, 0)
            is_live = slots < tile_count[grid_row, column]
            part = spread_tiles(source, tile_values[grid_row, column], block_column[grid_row, column],
                                block_row[grid_row, column], is_live, REGION_ROWS, False)
            return accum + lax.optimization_barrier(part.astype(jnp.bfloat16)).astype(jnp.float32)
        return lax.fori_loop(0, N_ROW, add_row, jnp.zeros((N_ROW * span, F), jnp.float32))

    hidden = lax.map(forward_group, jnp.arange(N_COL, dtype=jnp.int32)).reshape(NODES, F)
    activated = jax.nn.silu(hidden).astype(jnp.bfloat16)
    hidden_grad = (cotangent.astype(jnp.float32) * silu_slope(hidden)).astype(jnp.bfloat16)

    def backward_group(grid_row):
        def add_column(column, accum):
            first = (column * (N_ROW * span)).astype(jnp.int32)
            source = lax.dynamic_slice_in_dim(hidden_grad, first, N_ROW * span, 0)
            is_live = slots < tile_count[grid_row, column]
            part = spread_tiles(source, tile_values[grid_row, column], block_row[grid_row, column],
                                block_column[grid_row, column], is_live, REGION_COLS, True)
            return accum + lax.optimization_barrier(part.astype(jnp.bfloat16)).astype(jnp.float32)
        return lax.fori_loop(0, N_COL, add_column, jnp.zeros((N_COL * span, F), jnp.float32))

    feat_delta = lax.map(backward_group, jnp.arange(N_ROW, dtype=jnp.int32)).reshape(NODES, F).astype(jnp.bfloat16)
    feat_grad = jnp.dot(feat_delta, weight.T, preferred_element_type=jnp.float32).astype(jnp.bfloat16)
    weight_grad = jnp.dot(features.T, feat_delta, preferred_element_type=jnp.float32) * (NODES ** -0.5)
    return activated, feat_grad, weight_grad
```

```python
import functools

import jax
import jax.numpy as jnp
from jax import lax
from jax.experimental import pallas as pl
from jax.experimental.pallas import tpu as pltpu
from jax.sharding import PartitionSpec as P

BF16 = jnp.bfloat16
F32 = jnp.float32
VMEM_LIMIT = 56 * 2**20
SMEM_SPEC = pl.BlockSpec(memory_space=pltpu.SMEM)
VMEM_SPEC = pl.BlockSpec(memory_space=pltpu.VMEM)


class Grid:
    def __init__(self, rows, cols):
        self.R, self.C = rows, cols
        self.X = 2 if rows % 2 == 0 else 1
        self.K = 2 if cols % 2 == 0 else 1
        self.Z, self.Y = rows // self.X, cols // self.K

    def move(self, value, dz=0, dx=0, dy=0, dcore=0):
        pairs = []
        for z in range(self.Z):
            for x in range(self.X):
                for y in range(self.Y):
                    for k in range(self.K):
                        source = (z * self.X + x) * self.C + y * self.K + k
                        row = ((z + dz) % self.Z) * self.X + (x ^ dx)
                        col = ((y + dy) % self.Y) * self.K + (k ^ dcore)
                        pairs.append((source, row * self.C + col))
        return lax.ppermute(value, ("row", "col"), pairs)


def params(**more):
    return pltpu.CompilerParams(vmem_limit_bytes=VMEM_LIMIT, **more)


def build_kernel(g, slots, block, n_sources, *refs):
    place = refs[0]
    lists = refs[1 : 1 + n_sources]
    tiles = refs[1 + n_sources : 1 + 2 * n_sources]
    forward, backward = refs[1 + 2 * n_sources :]
    z, x, y, core = place[0], place[1], place[2], place[3]
    forward[...] = jnp.zeros_like(forward)
    backward[...] = jnp.zeros_like(backward)
    for source in range(n_sources):
        s_core, s_x = source // g.X, source % g.X
        listed, held = lists[source], tiles[source]

        @pl.loop(0, slots)
        def _(s):
            block_row, block_col = listed[s], listed[slots + s]
            z_out, x_out = lax.div(block_row, g.X), lax.rem(block_row, g.X)
            y_in, core_in = lax.div(block_col, g.K), lax.rem(block_col, g.K)
            dz = lax.rem(z_out - z + g.Z, g.Z)
            dy = lax.rem(y - y_in + g.Y, g.Y)
            dcore = jnp.where(core_in == core, 0, 1)
            live = jnp.logical_and(s < listed[2 * slots], x_out == x)
            if s_core == 0:

                @pl.when(live)
                def _():
                    at = s_x * g.C + dy * g.K + dcore
                    forward[
                        pl.ds(pl.multiple_of(dz * block, block), block),
                        pl.ds(pl.multiple_of(at * block, block), block),
                    ] = held[s]

            @pl.when(jnp.logical_and(live, dcore == 0))
            def _():
                out = s_x * g.Y + dy
                at = s_core * g.Z + dz
                backward[
                    pl.ds(pl.multiple_of(out * block, block), block),
                    pl.ds(pl.multiple_of(at * block, block), block),
                ] = held[s].astype(F32).T.astype(BF16)


def build(g, place, lists, tiles):
    slots, block = tiles[0].shape[0], tiles[0].shape[1]
    forward = (g.Z * block, g.X * g.C * block)
    backward = (g.X * g.Y * block, g.K * g.Z * block)
    return pl.pallas_call(
        functools.partial(build_kernel, g, slots, block, len(tiles)),
        out_shape=[jax.ShapeDtypeStruct(forward, BF16), jax.ShapeDtypeStruct(backward, BF16)],
        in_specs=[SMEM_SPEC] * (1 + len(lists)) + [VMEM_SPEC] * len(tiles),
        out_specs=[VMEM_SPEC] * 2,
        compiler_params=params(),
        name="build",
    )(place, *lists, *tiles)


def spread_kernel(n_in, block, matrix, *refs):
    stacked = jnp.concatenate([r[...] for r in refs[:n_in]], axis=0)
    total = jnp.dot(matrix[...], stacked, preferred_element_type=F32)
    for i, out in enumerate(refs[n_in:]):
        out[...] = total[i * block : (i + 1) * block].astype(BF16)


def spread(matrix, blocks, name):
    block, width = blocks[0].shape
    n_out = matrix.shape[0] // block
    tile = 256 if width % 256 == 0 else width
    spec = pl.BlockSpec((block, tile), lambda j: (0, j))
    return pl.pallas_call(
        functools.partial(spread_kernel, len(blocks), block),
        grid=(width // tile,),
        out_shape=[jax.ShapeDtypeStruct((block, width), BF16)] * n_out,
        in_specs=[pl.BlockSpec(matrix.shape, lambda j: (0, 0))] + [spec] * len(blocks),
        out_specs=[spec] * n_out,
        compiler_params=params(),
        cost_estimate=pl.CostEstimate(
            flops=2 * matrix.size * width,
            bytes_accessed=2 * (matrix.size + (len(blocks) + n_out) * block * width),
            transcendentals=0,
        ),
        name=name,
    )(matrix, *blocks)


def layer_kernel(n_in, place, *refs):
    parts = refs[:n_in]
    weight, cotangent = refs[n_in : n_in + 2]
    activated, hidden_grad, back, keep, send = refs[n_in + 2 : n_in + 7]
    agg, total = refs[n_in + 7 :]
    j, last = pl.program_id(0), pl.num_programs(0) - 1
    half = keep.shape[1]

    @pl.when(j == 0)
    def _():
        summed = parts[0][...].astype(F32)
        for part in parts[1:]:
            summed += part[...].astype(F32)
        agg[...] = summed.astype(BF16)
        total[...] = jnp.zeros_like(total)
        core = place[3]
        keep[...] = agg[:, pl.ds(pl.multiple_of(core * half, half), half)]
        send[...] = agg[:, pl.ds(pl.multiple_of((1 - core) * half, half), half)]

    hidden = jnp.dot(agg[...], weight[...], preferred_element_type=F32)
    sigmoid = jax.nn.sigmoid(hidden)
    activated[...] = (hidden * sigmoid).astype(BF16)
    slope = sigmoid * (1.0 + hidden * (1.0 - sigmoid))
    grad = (cotangent[...].astype(F32) * slope).astype(BF16)
    hidden_grad[...] = grad
    total[...] += lax.dot_general(
        grad, weight[...], (((1,), (1,)), ((), ())), preferred_element_type=F32
    )

    @pl.when(j == last)
    def _():
        back[...] = total[...].astype(BF16)


def layer(place, parts, weight, cotangent):
    rows, depth = parts[0].shape
    width = weight.shape[1]
    tile = 256 if width % 256 == 0 else width
    whole = pl.BlockSpec((rows, depth), lambda j: (0, 0))
    half = pl.BlockSpec((rows, depth // 2), lambda j: (0, 0))
    cut = pl.BlockSpec((rows, tile), lambda j: (0, j))
    return pl.pallas_call(
        functools.partial(layer_kernel, len(parts)),
        grid=(width // tile,),
        out_shape=[
            jax.ShapeDtypeStruct((rows, width), BF16),
            jax.ShapeDtypeStruct((rows, width), BF16),
            jax.ShapeDtypeStruct((rows, depth), BF16),
            jax.ShapeDtypeStruct((rows, depth // 2), BF16),
            jax.ShapeDtypeStruct((rows, depth // 2), BF16),
        ],
        in_specs=[SMEM_SPEC]
        + [whole] * len(parts)
        + [pl.BlockSpec((depth, tile), lambda j: (0, j)), cut],
        out_specs=[cut, cut, whole, half, half],
        scratch_shapes=[pltpu.VMEM((rows, depth), BF16), pltpu.VMEM((rows, depth), F32)],
        compiler_params=params(),
        cost_estimate=pl.CostEstimate(
            flops=4 * rows * depth * width,
            bytes_accessed=2 * (depth * width + 9 * rows * width),
            transcendentals=rows * width,
        ),
        name="layer",
    )(place, *parts, weight, cotangent)


def terms_kernel(g, place, keep, got, grad, grad_got, *refs):
    outs, turned = refs[:-1], refs[-1]
    both = jnp.concatenate([keep[...].astype(F32), got[...].astype(F32)], axis=0)
    turned[...] = both.T.astype(BF16)
    grads = jnp.concatenate([grad[...], grad_got[...]], axis=0)
    x, y = place[1], place[2]
    rows = outs[0].shape[0]
    for dx in range(g.X):
        for dy in range(g.Y):
            at = (x if dx == 0 else 1 - x) * g.Y + lax.rem(y + dy, g.Y)
            mine = turned[pl.ds(pl.multiple_of(at * rows, rows), rows), :]
            outs[dx * g.Y + dy][...] = jnp.dot(
                mine, grads, preferred_element_type=F32
            ).astype(BF16)


def terms(g, place, keep, got, grad, grad_got):
    nodes, half = keep.shape
    width = grad.shape[1]
    n_out = g.X * g.Y
    return pl.pallas_call(
        functools.partial(terms_kernel, g),
        out_shape=[jax.ShapeDtypeStruct((half // n_out, width), BF16)] * n_out,
        in_specs=[SMEM_SPEC] + [VMEM_SPEC] * 4,
        out_specs=[VMEM_SPEC] * n_out,
        scratch_shapes=[pltpu.VMEM((half, 2 * nodes), BF16)],
        compiler_params=params(),
        cost_estimate=pl.CostEstimate(
            flops=4 * nodes * half * width,
            bytes_accessed=2 * half * width,
            transcendentals=0,
        ),
        name="terms",
    )(place, keep, got, grad, grad_got)


def split_kernel(g, n_in, place, *refs):
    outs, held = refs[n_in:-1], refs[-1]
    summed = refs[0][...].astype(F32)
    for part in refs[1:n_in]:
        summed += part[...].astype(F32)
    held[...] = summed.astype(BF16)
    width = outs[0].shape[1]
    for k, out in enumerate(outs):
        at = lax.rem(place[0] + k, g.Z)
        out[...] = held[:, pl.ds(pl.multiple_of(at * width, width), width)]


def split(g, place, parts):
    rows, width = parts[0].shape
    return pl.pallas_call(
        functools.partial(split_kernel, g, len(parts)),
        out_shape=[jax.ShapeDtypeStruct((rows, width // g.Z), BF16)] * g.Z,
        in_specs=[SMEM_SPEC] + [VMEM_SPEC] * len(parts),
        out_specs=[VMEM_SPEC] * g.Z,
        scratch_shapes=[pltpu.VMEM((rows, width), BF16)],
        compiler_params=params(),
        name="split",
    )(place, *parts)


def join_kernel(g, place, *refs):
    out = refs[-1]
    rows, width = refs[0].shape[1], refs[0].shape[2]
    z, x, y, core = place[0], place[1], place[2], place[3]
    for dcore in range(g.K):
        for dx in range(g.X):
            for dy in range(g.Y):
                held = refs[(dcore * g.X + dx) * g.Y + dy]
                at_core = core if dcore == 0 else 1 - core
                at_x = x if dx == 0 else 1 - x
                at = (at_core * g.X + at_x) * g.Y + lax.rem(y - dy + g.Y, g.Y)
                for dz in range(g.Z):
                    col = lax.rem(z - dz + g.Z, g.Z)
                    out[
                        pl.ds(pl.multiple_of(at * rows, rows), rows),
                        pl.ds(pl.multiple_of(col * width, width), width),
                    ] = held[dz].astype(F32)


def join(g, place, pieces, shape):
    return pl.pallas_call(
        functools.partial(join_kernel, g),
        out_shape=jax.ShapeDtypeStruct(shape, F32),
        in_specs=[SMEM_SPEC] + [VMEM_SPEC] * len(pieces),
        out_specs=VMEM_SPEC,
        compiler_params=params(),
        name="join",
    )(place, *pieces)


def on_device(g, features, weight, cotangent, tile_values, block_row, block_column, tile_count):
    r, c = lax.axis_index("row"), lax.axis_index("col")
    place = jnp.stack([r // g.X, r % g.X, c // g.K, c % g.K]).astype(jnp.int32)
    squares = [(dx, dy) for dx in range(g.X) for dy in range(g.Y)]
    moves = [(dx, dy) for dx, dy in squares if (dx, dy) != (0, 0)]

    near = {(0, 0): features}
    for dx, dy in moves:
        near[dx, dy] = g.move(features, dx=dx, dy=dy)
    listed = jnp.concatenate([block_row[0, 0], block_column[0, 0], tile_count[0]])
    lists, tiles = [listed], [tile_values[0, 0]]
    if g.X == 2:
        lists.append(g.move(listed, dx=1))
        tiles.append(g.move(tiles[0], dx=1))
    if g.K == 2:
        lists += [g.move(v, dcore=1) for v in lists]
        tiles += [g.move(v, dcore=1) for v in tiles]
    forward, backward = build(g, place, lists, tiles)
    blocks = []
    for at in squares:
        blocks.append(near[at])
        if g.K == 2:
            blocks.append(g.move(near[at], dcore=1))

    sums = spread(forward, blocks, "spread_forward")
    parts = [sums[0]] + [g.move(sums[k], dz=k) for k in range(1, g.Z)]
    activated, hidden_grad, back, keep, send = layer(place, parts, weight, cotangent)

    mine = [back] + [None] * (g.Z - 1)
    for k in range(1, g.Z):
        mine[(g.Z - k) % g.Z] = g.move(back, dz=k)
    backs = list(mine)
    if g.K == 2:
        backs += [g.move(v, dcore=1) for v in mine]
    deltas = spread(backward, backs, "spread_backward")
    feat = deltas[0].astype(F32)
    for i, (dx, dy) in enumerate(squares):
        if (dx, dy) != (0, 0):
            feat += g.move(deltas[i], dx=dx, dy=-dy).astype(F32)
    feat_grad = feat.astype(BF16)

    got, grad_got = g.move(send, dcore=1), g.move(hidden_grad, dcore=1)
    shares = terms(g, place, keep, got, hidden_grad, grad_got)
    shares = [
        v if at == (0, 0) else g.move(v, dx=at[0], dy=at[1]) for at, v in zip(squares, shares)
    ]
    pieces = split(g, place, shares)
    total = pieces[0].astype(F32)
    for k in range(1, g.Z):
        total += g.move(pieces[k], dz=k).astype(F32)
    factor = (features.shape[0] * g.R * g.C) ** (-0.5)
    own = (total * factor).astype(BF16)
    column = jnp.stack([own] + [g.move(own, dz=k) for k in range(1, g.Z)])
    held = [column if at == (0, 0) else g.move(column, dx=at[0], dy=at[1]) for at in squares]
    if g.K == 2:
        held += [g.move(v, dcore=1) for v in held]
    weight_grad = join(g, place, held, weight.shape)
    return (activated, feat_grad, weight_grad)


def solution(mesh):
    g = Grid(mesh.shape["row"], mesh.shape["col"])
    return jax.shard_map(
        functools.partial(on_device, g),
        mesh=mesh,
        in_specs=(
            P(("row", "col"), None),
            P(),
            P(("col", "row"), None),
            P("row", "col", None, None, None),
            P("row", "col", None),
            P("row", "col", None),
            P("row", "col"),
        ),
        out_specs=(P(("col", "row"), None), P(("row", "col"), None), P()),
        check_vma=False,
    )
```

```python
import functools

import jax
import jax.numpy as jnp
from jax import lax
from jax.experimental import pallas as pl
from jax.experimental.pallas import tpu as pltpu
from jax.sharding import PartitionSpec as P

BF16 = jnp.bfloat16
F32 = jnp.float32
VMEM_LIMIT = 56 * 2**20
SMEM_SPEC = pl.BlockSpec(memory_space=pltpu.SMEM)
VMEM_SPEC = pl.BlockSpec(memory_space=pltpu.VMEM)


COST = {}


def cost(name):
    return pl.CostEstimate(flops=0, bytes_accessed=COST.get(name, 0), transcendentals=0)


class Grid:
    def __init__(self, rows, cols):
        if rows & (rows - 1) or cols & (cols - 1) or min(rows, cols) < 2:
            raise ValueError("mesh axes")
        self.R, self.C = rows, cols
        self.X, self.K = 2, 2
        self.Z, self.Y = rows // 2, cols // 2

    def devices(self):
        for z in range(self.Z):
            for x in range(self.X):
                for y in range(self.Y):
                    for k in range(self.K):
                        yield z, x, y, k

    def index(self, z, x, y, k):
        return (z * self.X + x) * self.C + y * self.K + k

    def move(self, value, dz=0, dx=0, dy=0, dk=0):
        pairs = [
            (self.index(z, x, y, k), self.index(z ^ dz, x ^ dx, y ^ dy, k ^ dk))
            for z, x, y, k in self.devices()
        ]
        return lax.ppermute(value, ("row", "col"), pairs)

    def along(self, value, hops):
        pairs = [
            (self.index(z, x, y, k), self.index(hops[z], x, y, k))
            for z, x, y, k in self.devices()
            if z in hops
        ]
        return lax.ppermute(value, ("row", "col"), pairs)

    def here(self):
        r, c = lax.axis_index("row"), lax.axis_index("col")
        return r // 2, r % 2, c // 2, c % 2


def params(**more):
    return pltpu.CompilerParams(vmem_limit_bytes=VMEM_LIMIT, **more)


def add_tiles(g, out, held, listed, slots, block, place):
    block_rows, block_cols, count = listed

    def one(s):
        wanted, row, col, turned = place(block_rows(s), block_cols(s))

        @pl.when(jnp.logical_and(s < count(), wanted))
        def _():
            tile = held[s]
            if turned:
                tile = tile.astype(F32).T.astype(BF16)
            out[
                pl.ds(pl.multiple_of(row * block, block), block),
                pl.ds(pl.multiple_of(col * block, block), block),
            ] = tile

    if slots <= 16:
        for s in range(slots):
            one(s)
    else:
        pl.loop(0, slots)(one)


def reader(listed, slots):
    return (lambda s: listed[s]), (lambda s: listed[slots + s]), (lambda: listed[2 * slots])


def multiply(matrix, stacked, outs, block):
    width = stacked.shape[1]
    tile = 256 if width % 256 == 0 else width

    def one(j):
        cols = pl.ds(j * tile if isinstance(j, int) else pl.multiple_of(j * tile, tile), tile)
        total = jnp.dot(matrix[...], stacked[:, cols], preferred_element_type=F32)
        for i, out in enumerate(outs):
            out[:, cols] = total[i * block : (i + 1) * block].astype(BF16)

    if matrix.shape[0] * matrix.shape[1] <= 2**20:
        for j in range(width // tile):
            one(j)
    else:
        pl.loop(0, width // tile)(one)


def forward_kernel(g, slots, block, n_in, *refs):
    lists, tiles = refs[:2], refs[2:4]
    blocks, outs = refs[4 : 4 + n_in], refs[4 + n_in : 4 + n_in + g.Z]
    matrix, stacked = refs[4 + n_in + g.Z :]
    z, x, y, k = g.here()
    matrix[...] = jnp.zeros_like(matrix)
    for dx in range(g.X):

        def place(row, col, dx=dx):
            at_z, at_x = row // g.X, row % g.X
            at_y, at_k = col // g.K, col % g.K
            at = dx * g.C + (at_y ^ y) * g.K + (at_k ^ k)
            return at_x == x, at_z ^ z, at, False

        add_tiles(g, matrix, tiles[dx], reader(lists[dx], slots), slots, block, place)
    for i, held in enumerate(blocks):
        stacked[pl.ds(i * block, block), :] = held[...]
    multiply(matrix, stacked, outs, block)


def forward(g, lists, tiles, blocks):
    slots = tiles[0].shape[0]
    block, width = blocks[0].shape
    n = len(blocks)
    return pl.pallas_call(
        functools.partial(forward_kernel, g, slots, block, n),
        out_shape=[jax.ShapeDtypeStruct((block, width), BF16)] * g.Z,
        in_specs=[SMEM_SPEC] * 2 + [VMEM_SPEC] * (2 + n),
        out_specs=[VMEM_SPEC] * g.Z,
        scratch_shapes=[
            pltpu.VMEM((g.Z * block, n * block), BF16),
            pltpu.VMEM((n * block, width), BF16),
        ],
        compiler_params=params(),
        cost_estimate=cost("forward"),
        name="forward",
    )(*lists, *tiles, *blocks)


def build_kernel(g, slots, block, *refs):
    lists, tiles, bundle, matrix = refs[:4], refs[4:6], refs[6], refs[7]
    z, x, y, k = g.here()
    matrix[...] = jnp.zeros_like(matrix)
    for dk in range(g.K):
        for dx in range(g.X):

            def place(row, col, dk=dk, dx=dx):
                at_z, at_x = row // g.X, row % g.X
                at_y, at_k = col // g.K, col % g.K
                wanted = jnp.logical_and(at_x == x, at_k == k)
                return wanted, dx * g.Y + (at_y ^ y), dk * g.Z + (at_z ^ z), True

            held = tiles[dx] if dk == 0 else bundle.at[pl.ds(dx * slots, slots)]
            listed = reader(lists[dk * g.X + dx], slots)
            add_tiles(g, matrix, held, listed, slots, block, place)


def build(g, lists, tiles, bundle):
    slots, block = tiles[0].shape[0], tiles[0].shape[1]
    return pl.pallas_call(
        functools.partial(build_kernel, g, slots, block),
        out_shape=jax.ShapeDtypeStruct((g.X * g.Y * block, g.K * g.Z * block), BF16),
        in_specs=[SMEM_SPEC] * 4 + [VMEM_SPEC] * 3,
        out_specs=VMEM_SPEC,
        compiler_params=params(),
        cost_estimate=cost("build"),
        name="build",
    )(*lists, *tiles, bundle)


def backward_kernel(g, block, groups, matrix, *refs):
    n_in = sum(groups)
    outs, stacked = refs[n_in:-1], refs[-1]
    at = 0
    for i, n in enumerate(groups):
        held = refs[at][...]
        for more in refs[at + 1 : at + n]:
            held = held + more[...]
        stacked[pl.ds(i * block, block), :] = held
        at += n
    multiply(matrix, stacked, outs, block)


def backward(g, matrix, groups):
    block, width = groups[0][0].shape
    n_out = matrix.shape[0] // block
    flat = [v for group in groups for v in group]
    return pl.pallas_call(
        functools.partial(backward_kernel, g, block, [len(group) for group in groups]),
        out_shape=[jax.ShapeDtypeStruct((block, width), BF16)] * n_out,
        in_specs=[VMEM_SPEC] * (1 + len(flat)),
        out_specs=[VMEM_SPEC] * n_out,
        scratch_shapes=[pltpu.VMEM((len(groups) * block, width), BF16)],
        compiler_params=params(),
        cost_estimate=cost("backward"),
        name="backward",
    )(matrix, *flat)


def fold(g, split):
    total = split[0].astype(F32)
    for i in range(1, g.X * g.Y):
        total += g.move(split[i], dx=i // g.Y, dy=i % g.Y).astype(F32)
    return total


def layer_kernel(g, n_in, *refs):
    parts = refs[:n_in]
    weight, cotangent = refs[n_in : n_in + 2]
    activated, share, back, keep = refs[n_in + 2 : n_in + 6]
    agg, total = refs[n_in + 6 :]
    j, last = pl.program_id(0), pl.num_programs(0) - 1
    half = keep.shape[1]

    @pl.when(j == 0)
    def _():
        summed = parts[0][...].astype(F32)
        for part in parts[1:]:
            summed += part[...].astype(F32)
        agg[...] = summed.astype(BF16)
        total[...] = jnp.zeros_like(total)
        core = g.here()[3]
        keep[...] = agg[:, pl.ds(pl.multiple_of(core * half, half), half)]
        share[:, :half] = agg[:, pl.ds(pl.multiple_of((1 - core) * half, half), half)]

    hidden = jnp.dot(agg[...], weight[...], preferred_element_type=F32)
    sigmoid = jax.nn.sigmoid(hidden)
    activated[...] = (hidden * sigmoid).astype(BF16)
    slope = sigmoid * (1.0 + hidden * (1.0 - sigmoid))
    grad = (cotangent[...].astype(F32) * slope).astype(BF16)
    share[:, pl.ds(pl.multiple_of(half + j * grad.shape[1], grad.shape[1]), grad.shape[1])] = grad
    total[...] += lax.dot_general(
        grad, weight[...], (((1,), (1,)), ((), ())), preferred_element_type=F32
    )

    @pl.when(j == last)
    def _():
        back[...] = total[...].astype(BF16)


def layer(g, parts, weight, cotangent):
    rows, depth = parts[0].shape
    width = weight.shape[1]
    tile = 256 if width % 256 == 0 else width
    whole = pl.BlockSpec((rows, depth), lambda j: (0, 0))
    half = pl.BlockSpec((rows, depth // 2), lambda j: (0, 0))
    shared = pl.BlockSpec((rows, depth // 2 + width), lambda j: (0, 0))
    cut = pl.BlockSpec((rows, tile), lambda j: (0, j))
    return pl.pallas_call(
        functools.partial(layer_kernel, g, len(parts)),
        grid=(width // tile,),
        out_shape=[
            jax.ShapeDtypeStruct((rows, width), BF16),
            jax.ShapeDtypeStruct((rows, depth // 2 + width), BF16),
            jax.ShapeDtypeStruct((rows, depth), BF16),
            jax.ShapeDtypeStruct((rows, depth // 2), BF16),
        ],
        in_specs=[whole] * len(parts)
        + [pl.BlockSpec((depth, tile), lambda j: (0, j)), cut],
        out_specs=[cut, shared, whole, half],
        scratch_shapes=[pltpu.VMEM((rows, depth), BF16), pltpu.VMEM((rows, depth), F32)],
        compiler_params=params(),
        cost_estimate=cost("layer"),
        name="layer",
    )(*parts, weight, cotangent)


def terms_kernel(g, keep, share, share_got, *refs):
    outs, turned, grads = refs[:-2], refs[-2], refs[-1]
    nodes, half = keep.shape
    both = jnp.concatenate([keep[...].astype(F32), share_got[:, :half].astype(F32)], axis=0)
    turned[...] = both.T.astype(BF16)
    z, x, y, _ = g.here()
    rows, width = outs[0].shape[1:]
    for dz in range(g.Z):
        cols = pl.ds(pl.multiple_of(half + (z ^ dz) * width, width), width)
        grads[0:nodes, dz * width : (dz + 1) * width] = share[:, cols]
        grads[nodes:, dz * width : (dz + 1) * width] = share_got[:, cols]
    for dx in range(g.X):
        for dy in range(g.Y):
            at = (x ^ dx) * g.Y + (y ^ dy)
            mine = turned[pl.ds(pl.multiple_of(at * rows, rows), rows), :]
            total = jnp.dot(mine, grads[...], preferred_element_type=F32).astype(BF16)
            for dz in range(g.Z):
                outs[dx * g.Y + dy][dz] = total[:, dz * width : (dz + 1) * width]


def terms(g, keep, share, share_got):
    nodes, half = keep.shape
    width = share.shape[1] - half
    n_out = g.X * g.Y
    shapes = [jax.ShapeDtypeStruct((g.Z, half // n_out, width // g.Z), BF16)] * n_out
    return pl.pallas_call(
        functools.partial(terms_kernel, g),
        out_shape=shapes,
        in_specs=[VMEM_SPEC] * 3,
        out_specs=[VMEM_SPEC] * len(shapes),
        scratch_shapes=[
            pltpu.VMEM((half, 2 * nodes), BF16),
            pltpu.VMEM((2 * nodes, width), BF16),
        ],
        compiler_params=params(),
        cost_estimate=cost("terms"),
        name="terms",
    )(keep, share, share_got)


def join_kernel(g, places, *refs):
    out = refs[-1]
    rows, width = refs[0].shape[1:]
    z, x, y, k = g.here()
    for (dk, dx, dy, first), held in zip(places, refs):
        at = ((k ^ dk) * g.X + (x ^ dx)) * g.Y + (y ^ dy)
        for i in range(held.shape[0]):
            col = z ^ (first + i)
            out[
                pl.ds(pl.multiple_of(at * rows, rows), rows),
                pl.ds(pl.multiple_of(col * width, width), width),
            ] = held[i].astype(F32)


def join(g, places, pieces, shape):
    return pl.pallas_call(
        functools.partial(join_kernel, g, places),
        out_shape=jax.ShapeDtypeStruct(shape, F32),
        in_specs=[VMEM_SPEC] * len(pieces),
        out_specs=VMEM_SPEC,
        compiler_params=params(),
        cost_estimate=cost("join"),
        name="join",
    )(*pieces)


def on_device(g, features, weight, cotangent, tile_values, block_row, block_column, tile_count):
    pin = lax.optimization_barrier

    def after(value, *others):
        return pin((value, others))[0]

    squares = [(dx, dy) for dx in range(g.X) for dy in range(g.Y)]

    listed = jnp.concatenate([block_row[0, 0], block_column[0, 0], tile_count[0]])
    lists = [listed, g.move(listed, dx=1)]
    tiles = [tile_values[0, 0], g.move(after(tile_values[0, 0], listed), dx=1)]
    near = {(0, 0): features}
    for dx, dy in squares[1:]:
        near[dx, dy] = g.move(after(features, listed), dx=dx, dy=dy)
    blocks = []
    for at in squares:
        value = near[at] if at != (0, 0) else after(features, near[1, 0])
        blocks += [near[at], g.move(value, dk=1)]
    sums = forward(g, lists, tiles, blocks)
    parts = [sums[0]] + [g.move(sums[dz], dz=dz) for dz in range(1, g.Z)]

    slots, block = tiles[0].shape[:2]
    rows = [jnp.broadcast_to(v, slots) for at in lists for v in (at[:slots], at[slots:-1], at[-1])]
    codes = jnp.pad(jnp.stack(rows).astype(BF16), ((0, block - len(rows)), (0, block - slots)))[None]
    bundle = g.move(jnp.concatenate(after(tiles, sums) + [codes], axis=0), dk=1)
    got = bundle[2 * slots, : len(rows), :slots].astype(jnp.int32)
    others = [jnp.concatenate([got[i], got[i + 1], got[i + 2, :1]]) for i in (0, 3)]
    matrix = build(g, lists + others, tiles, bundle)
    parts, matrix = pin((parts, matrix))
    activated, share, back, keep = layer(g, parts, weight, cotangent)

    shares = terms(g, keep, share, g.move(share, dk=1))

    if g.Z == 0:
        far = g.move(back, dz=2)
        far = after(far, shares)
        groups = [[back], [g.move(back, dz=1)], [far]]
        groups.append([g.along(back, {1: 2, 2: 1}), g.along(far, {1: 0, 2: 3})])
    else:
        groups = [[back]] + [[g.move(back, dz=dz)] for dz in range(1, g.Z)]
    arrived = groups[1:]
    groups += [[g.move(v, dk=1) for v in group] for group in groups]
    deltas = backward(g, matrix, groups)
    feat_grad = fold(g, deltas).astype(BF16)

    pieces = after(fold(g, shares).astype(BF16), arrived)
    total = pieces[0].astype(F32)
    for dz in range(1, g.Z):
        total += g.move(pieces[dz], dz=dz).astype(F32)
    factor = (features.shape[0] * g.R * g.C) ** (-0.5)
    own = (total * factor).astype(BF16)
    column = jnp.stack([own] + [g.move(own, dz=dz) for dz in range(1, g.Z)])
    column = after(column, deltas)
    held = [column if at == (0, 0) else g.move(column, dx=at[0], dy=at[1]) for at in squares]
    held += [g.move(v, dk=1) for v in held]
    places = [(dk, *at, 0) for dk in range(g.K) for at in squares]
    weight_grad = join(g, places, held, weight.shape)
    return (activated, feat_grad, weight_grad)


def solution(mesh):
    g = Grid(mesh.shape["row"], mesh.shape["col"])
    return jax.shard_map(
        functools.partial(on_device, g),
        mesh=mesh,
        in_specs=(
            P(("row", "col"), None),
            P(),
            P(("col", "row"), None),
            P("row", "col", None, None, None),
            P("row", "col", None),
            P("row", "col", None),
            P("row", "col"),
        ),
        out_specs=(P(("col", "row"), None), P(("row", "col"), None), P()),
        check_vma=False,
    )
```

```python
import functools

import jax
import jax.numpy as jnp
from jax import lax
from jax.experimental import pallas as pl
from jax.experimental.pallas import tpu as pltpu
from jax.sharding import PartitionSpec as P

BF16 = jnp.bfloat16
F32 = jnp.float32
VMEM_LIMIT = 56 * 2**20
SMEM_SPEC = pl.BlockSpec(memory_space=pltpu.SMEM)
VMEM_SPEC = pl.BlockSpec(memory_space=pltpu.VMEM)
HBM_SPEC = pl.BlockSpec(memory_space=pl.ANY)


COST = {}


def cost(name):
    return pl.CostEstimate(flops=0, bytes_accessed=COST.get(name, 0), transcendentals=0)


class Grid:
    def __init__(self, rows, cols):
        if rows & (rows - 1) or cols & (cols - 1) or min(rows, cols) < 2:
            raise ValueError("mesh axes")
        self.R, self.C = rows, cols
        self.X, self.K = 2, 2
        self.Z, self.Y = rows // 2, cols // 2

    def devices(self):
        for z in range(self.Z):
            for x in range(self.X):
                for y in range(self.Y):
                    for k in range(self.K):
                        yield z, x, y, k

    def index(self, z, x, y, k):
        return (z * self.X + x) * self.C + y * self.K + k

    def move(self, value, dz=0, dx=0, dy=0, dk=0):
        pairs = [
            (self.index(z, x, y, k), self.index(z ^ dz, x ^ dx, y ^ dy, k ^ dk))
            for z, x, y, k in self.devices()
        ]
        return lax.ppermute(value, ("row", "col"), pairs)

    def swap_xy(self, value):
        groups = [
            [self.index(z, x, y, k) for x in range(self.X) for y in range(self.Y)]
            for z in range(self.Z)
            for k in range(self.K)
        ]
        return lax.all_to_all(value, ("row", "col"), 0, 0, axis_index_groups=groups, tiled=True)

    def here(self):
        r, c = lax.axis_index("row"), lax.axis_index("col")
        return r // 2, r % 2, c // 2, c % 2


def params(**more):
    return pltpu.CompilerParams(vmem_limit_bytes=VMEM_LIMIT, **more)


def add_tiles(g, out, held, listed, slots, block, place):
    block_rows, block_cols, count = listed

    def one(s):
        wanted, row, col, turned = place(block_rows(s), block_cols(s))

        @pl.when(jnp.logical_and(s < count(), wanted))
        def _():
            tile = held[s]
            if turned:
                tile = tile.astype(F32).T.astype(BF16)
            out[
                pl.ds(pl.multiple_of(row * block, block), block),
                pl.ds(pl.multiple_of(col * block, block), block),
            ] = tile

    if slots <= 16:
        for s in range(slots):
            one(s)
    else:
        pl.loop(0, slots)(one)


def reader(listed, slots, at=0):
    first = at * (2 * slots + 1)
    return (
        lambda s: listed[first + s],
        lambda s: listed[first + slots + s],
        lambda: listed[first + 2 * slots],
    )


def multiply(matrix, stacked, outs, block):
    width = stacked.shape[1]
    tile = 256 if width % 256 == 0 else width

    def one(j):
        cols = pl.ds(j * tile if isinstance(j, int) else pl.multiple_of(j * tile, tile), tile)
        total = jnp.dot(matrix[...], stacked[:, cols], preferred_element_type=F32)
        for i, out in enumerate(outs):
            out[:, cols] = total[i * block : (i + 1) * block].astype(BF16)

    if matrix.shape[0] * matrix.shape[1] <= 2**20:
        for j in range(width // tile):
            one(j)
    else:
        pl.loop(0, width // tile)(one)


def forward_kernel(g, slots, block, n_in, *refs):
    lists, tiles = refs[:2], refs[2:4]
    blocks, outs = refs[4 : 4 + n_in], refs[4 + n_in : 4 + n_in + g.Z]
    matrix, stacked = refs[4 + n_in + g.Z :]
    z, x, y, k = g.here()
    matrix[...] = jnp.zeros_like(matrix)
    for dx in range(g.X):

        def place(row, col, dx=dx):
            at_z, at_x = row // g.X, row % g.X
            at_y, at_k = col // g.K, col % g.K
            at = dx * g.C + (at_y ^ y) * g.K + (at_k ^ k)
            return at_x == x, at_z ^ z, at, False

        add_tiles(g, matrix, tiles[dx], reader(lists[dx], slots), slots, block, place)
    for i, held in enumerate(blocks):
        stacked[pl.ds(i * block, block), :] = held[...]
    multiply(matrix, stacked, outs, block)


def forward(g, lists, tiles, blocks):
    slots = tiles[0].shape[0]
    block, width = blocks[0].shape
    n = len(blocks)
    return pl.pallas_call(
        functools.partial(forward_kernel, g, slots, block, n),
        out_shape=[jax.ShapeDtypeStruct((block, width), BF16)] * g.Z,
        in_specs=[SMEM_SPEC] * 2 + [VMEM_SPEC] * (2 + n),
        out_specs=[VMEM_SPEC] * g.Z,
        scratch_shapes=[
            pltpu.VMEM((g.Z * block, n * block), BF16),
            pltpu.VMEM((n * block, width), BF16),
        ],
        compiler_params=params(),
        cost_estimate=cost("forward"),
        name="forward",
    )(*lists, *tiles, *blocks)


def build_kernel(g, slots, block, *refs):
    lists, tiles, matrix = refs[:3], refs[3:7], refs[7]
    z, x, y, k = g.here()
    matrix[...] = jnp.zeros_like(matrix)
    for dk in range(g.K):
        for dx in range(g.X):

            def place(row, col, dk=dk, dx=dx):
                at_z, at_x = row // g.X, row % g.X
                at_y, at_k = col // g.K, col % g.K
                wanted = jnp.logical_and(at_x == x, at_k == k)
                return wanted, (x ^ dx) * g.Y + at_y, dk * g.Z + (at_z ^ z), True

            listed = reader(lists[2], slots, dx) if dk else reader(lists[dx], slots)
            add_tiles(g, matrix, tiles[dk * g.X + dx], listed, slots, block, place)


def build(g, lists, tiles):
    slots, block = tiles[0].shape[0], tiles[0].shape[1]
    return pl.pallas_call(
        functools.partial(build_kernel, g, slots, block),
        out_shape=jax.ShapeDtypeStruct((g.X * g.Y * block, g.K * g.Z * block), BF16),
        in_specs=[SMEM_SPEC] * 3 + [VMEM_SPEC] * 4,
        out_specs=VMEM_SPEC,
        compiler_params=params(),
        cost_estimate=cost("build"),
        name="build",
    )(*lists, *tiles)


def backward_kernel(g, block, groups, matrix, *refs):
    n_in = sum(groups)
    out, stacked = refs[n_in:]
    outs = [out.at[pl.ds(i * block, block)] for i in range(matrix.shape[0] // block)]
    at = 0
    for i, n in enumerate(groups):
        held = refs[at][...]
        for more in refs[at + 1 : at + n]:
            held = held + more[...]
        stacked[pl.ds(i * block, block), :] = held
        at += n
    multiply(matrix, stacked, outs, block)


def backward(g, matrix, groups):
    block, width = groups[0][0].shape
    flat = [v for group in groups for v in group]
    return pl.pallas_call(
        functools.partial(backward_kernel, g, block, [len(group) for group in groups]),
        out_shape=jax.ShapeDtypeStruct((matrix.shape[0], width), BF16),
        in_specs=[VMEM_SPEC] * (1 + len(flat)),
        out_specs=VMEM_SPEC,
        scratch_shapes=[pltpu.VMEM((len(groups) * block, width), BF16)],
        compiler_params=params(),
        cost_estimate=cost("backward"),
        name="backward",
    )(matrix, *flat)


def fold(g, split):
    total = split[0].astype(F32)
    for i in range(1, g.X * g.Y):
        total += g.move(split[i], dx=i // g.Y, dy=i % g.Y).astype(F32)
    return total


def layer_kernel(g, n_in, *refs):
    parts = refs[:n_in]
    weight, cotangent = refs[n_in : n_in + 2]
    activated, share, back, keep = refs[n_in + 2 : n_in + 6]
    agg = refs[n_in + 6]
    half = keep.shape[1]
    summed = parts[0][...].astype(F32)
    for part in parts[1:]:
        summed += part[...].astype(F32)
    agg[...] = summed.astype(BF16)
    core = g.here()[3]
    keep[...] = agg[:, pl.ds(pl.multiple_of(core * half, half), half)]
    share[:, :half] = agg[:, pl.ds(pl.multiple_of((1 - core) * half, half), half)]
    width = weight.shape[1]
    tile = 256 if width % 256 == 0 else width
    for j in range(width // tile):
        cols = slice(j * tile, (j + 1) * tile)
        hidden = jnp.dot(agg[...], weight[:, cols], preferred_element_type=F32)
        sigmoid = jax.nn.sigmoid(hidden)
        activated[:, cols] = (hidden * sigmoid).astype(BF16)
        slope = sigmoid * (1.0 + hidden * (1.0 - sigmoid))
        grad = (cotangent[:, cols].astype(F32) * slope).astype(BF16)
        share[:, half + j * tile : half + (j + 1) * tile] = grad
    back[...] = lax.dot_general(
        share[:, half:], weight[...], (((1,), (1,)), ((), ())), preferred_element_type=F32
    ).astype(BF16)


def layer(g, parts, weight, cotangent):
    rows, depth = parts[0].shape
    width = weight.shape[1]
    return pl.pallas_call(
        functools.partial(layer_kernel, g, len(parts)),
        out_shape=[
            jax.ShapeDtypeStruct((rows, width), BF16),
            jax.ShapeDtypeStruct((rows, depth // 2 + width), BF16),
            jax.ShapeDtypeStruct((rows, depth), BF16),
            jax.ShapeDtypeStruct((rows, depth // 2), BF16),
        ],
        in_specs=[VMEM_SPEC] * (len(parts) + 2),
        out_specs=[VMEM_SPEC] * 4,
        scratch_shapes=[pltpu.VMEM((rows, depth), BF16)],
        compiler_params=params(),
        cost_estimate=cost("layer"),
        name="layer",
    )(*parts, weight, cotangent)


def terms_kernel(g, keep, share, share_got, *refs):
    outs, turned, grads = refs[:-2], refs[-2], refs[-1]
    nodes, half = keep.shape
    both = jnp.concatenate([keep[...].astype(F32), share_got[:, :half].astype(F32)], axis=0)
    turned[...] = both.T.astype(BF16)
    z, x, y, _ = g.here()
    rows, width = outs[0].shape[1:]
    for dz in range(g.Z):
        cols = pl.ds(pl.multiple_of(half + (z ^ dz) * width, width), width)
        grads[0:nodes, dz * width : (dz + 1) * width] = share[:, cols]
        grads[nodes:, dz * width : (dz + 1) * width] = share_got[:, cols]
    for dx in range(g.X):
        for dy in range(g.Y):
            at = (x ^ dx) * g.Y + (y ^ dy)
            mine = turned[pl.ds(pl.multiple_of(at * rows, rows), rows), :]
            total = jnp.dot(mine, grads[...], preferred_element_type=F32).astype(BF16)
            for dz in range(g.Z):
                outs[dx * g.Y + dy][dz] = total[:, dz * width : (dz + 1) * width]


def terms(g, keep, share, share_got):
    nodes, half = keep.shape
    width = share.shape[1] - half
    n_out = g.X * g.Y
    shapes = [jax.ShapeDtypeStruct((g.Z, half // n_out, width // g.Z), BF16)] * n_out
    return pl.pallas_call(
        functools.partial(terms_kernel, g),
        out_shape=shapes,
        in_specs=[VMEM_SPEC] * 3,
        out_specs=[VMEM_SPEC] * len(shapes),
        scratch_shapes=[
            pltpu.VMEM((half, 2 * nodes), BF16),
            pltpu.VMEM((2 * nodes, width), BF16),
        ],
        compiler_params=params(),
        cost_estimate=cost("terms"),
        name="terms",
    )(keep, share, share_got)


def join_kernel(g, places, *refs):
    n = len(places)
    pieces, out = refs[:n], refs[n]
    held, whole, in_sems, out_sems = refs[n + 1 :]
    some, rows, width = pieces[0].shape
    z, x, y, k = g.here()
    copies = [pltpu.make_async_copy(v, held.at[i], in_sems.at[i]) for i, v in enumerate(pieces)]
    for copy in copies:
        copy.start()
    sent = []
    for i, (dk, dx, dy) in enumerate(places):
        copies[i].wait()
        at = ((k ^ dk) * g.X + (x ^ dx)) * g.Y + (y ^ dy)
        at = pl.ds(pl.multiple_of(at * rows, rows), rows)
        for dz in range(some):
            cols = pl.ds(pl.multiple_of((z ^ dz) * width, width), width)
            whole[i, :, cols] = held[i, dz].astype(F32)
        copy = pltpu.make_async_copy(whole.at[i], out.at[at], out_sems.at[i])
        copy.start()
        sent.append(copy)
    for copy in sent:
        copy.wait()


def join(g, places, pieces, shape):
    n = len(pieces)
    some, rows, width = pieces[0].shape
    return pl.pallas_call(
        functools.partial(join_kernel, g, places),
        out_shape=jax.ShapeDtypeStruct(shape, F32),
        in_specs=[HBM_SPEC] * n,
        out_specs=HBM_SPEC,
        scratch_shapes=[
            pltpu.VMEM((n, some, rows, width), BF16),
            pltpu.VMEM((n, rows, some * width), F32),
            pltpu.SemaphoreType.DMA((n,)),
            pltpu.SemaphoreType.DMA((n,)),
        ],
        compiler_params=params(),
        cost_estimate=cost("join"),
        name="join",
    )(*pieces)


def on_device(g, features, weight, cotangent, tile_values, block_row, block_column, tile_count):
    pin = lax.optimization_barrier

    def after(value, *others):
        return pin((value, others))[0]

    squares = [(dx, dy) for dx in range(g.X) for dy in range(g.Y)]

    listed = jnp.concatenate([block_row[0, 0], block_column[0, 0], tile_count[0]])
    lists = [listed, g.move(listed, dx=1)]
    tiles = [tile_values[0, 0], g.move(after(tile_values[0, 0], listed), dx=1)]
    near = {(0, 0): features}
    for dx, dy in [(1, 0)] + [at for at in squares[1:] if at != (1, 0)]:
        if dx and dy:
            near[dx, dy] = g.move(after(near[1, 0], lists[1]), dy=dy)
        else:
            near[dx, dy] = g.move(after(features, listed), dx=dx, dy=dy)
    blocks = []
    for at in squares:
        value = near[at] if at != (0, 0) else after(features, near[1, 0])
        blocks += [near[at], g.move(value, dk=1)]
    others = [g.move(after(tiles[0], near[1, 0]), dk=1)]
    lists.append(g.move(jnp.concatenate(lists), dk=1))
    blocks[0] = after(blocks[0], (others, lists[2]))
    sums = forward(g, lists[:2], tiles, blocks)
    parts = [sums[0]] + [g.move(sums[dz], dz=dz) for dz in range(1, g.Z)]
    others.append(g.move(after(tiles[1], sums), dk=1))
    matrix = build(g, lists, tiles + others)
    parts, matrix = pin((parts, matrix))
    activated, share, back, keep = layer(g, parts, weight, cotangent)

    shares = terms(g, keep, share, g.move(share, dk=1))

    groups = [[back]] + [[g.move(back, dz=dz)] for dz in range(1, g.Z)]
    arrived = groups[1:]
    groups += [[g.move(v, dk=1) for v in group] for group in groups]
    deltas = backward(g, matrix, groups)
    feat = g.swap_xy(deltas).astype(F32).reshape(g.X * g.Y, -1, deltas.shape[1])
    feat_grad = jnp.sum(feat, axis=0).astype(BF16)

    pieces = after(fold(g, shares).astype(BF16), arrived)
    total = pieces[0].astype(F32)
    for dz in range(1, g.Z):
        total += g.move(pieces[dz], dz=dz).astype(F32)
    factor = (features.shape[0] * g.R * g.C) ** (-0.5)
    own = (total * factor).astype(BF16)
    column = jnp.stack([own] + [g.move(own, dz=dz) for dz in range(1, g.Z)])
    column = after(column, deltas)
    held = [column if at == (0, 0) else g.move(column, dx=at[0], dy=at[1]) for at in squares]
    held += [g.move(v, dk=1) for v in held]
    places = [(dk, *at) for dk in range(g.K) for at in squares]
    held[-1] = after(held[-1], feat_grad)
    weight_grad = join(g, places, held, weight.shape)
    return (activated, feat_grad, weight_grad)


def solution(mesh):
    g = Grid(mesh.shape["row"], mesh.shape["col"])
    return jax.shard_map(
        functools.partial(on_device, g),
        mesh=mesh,
        in_specs=(
            P(("row", "col"), None),
            P(),
            P(("col", "row"), None),
            P("row", "col", None, None, None),
            P("row", "col", None),
            P("row", "col", None),
            P("row", "col"),
        ),
        out_specs=(P(("col", "row"), None), P(("row", "col"), None), P()),
        check_vma=False,
    )
```

```python
import functools

import jax
import jax.numpy as jnp
from jax import lax
from jax.experimental import pallas as pl
from jax.experimental.pallas import tpu as pltpu
from jax.sharding import PartitionSpec as P

BF16 = jnp.bfloat16
F32 = jnp.float32
VMEM_LIMIT = 64 * 2**20 - 2**18
SMEM_SPEC = pl.BlockSpec(memory_space=pltpu.SMEM)
VMEM_SPEC = pl.BlockSpec(memory_space=pltpu.VMEM)
HBM_SPEC = pl.BlockSpec(memory_space=pl.ANY)


COST = {}


def cost(name):
    return pl.CostEstimate(flops=0, bytes_accessed=COST.get(name, 0), transcendentals=0)


class Grid:
    def __init__(self, rows, cols):
        if rows & (rows - 1) or cols & (cols - 1) or min(rows, cols) < 2:
            raise ValueError("mesh axes")
        self.R, self.C = rows, cols
        self.X, self.K = 2, 2
        self.Z, self.Y = rows // 2, cols // 2

    def devices(self):
        for z in range(self.Z):
            for x in range(self.X):
                for y in range(self.Y):
                    for k in range(self.K):
                        yield z, x, y, k

    def index(self, z, x, y, k):
        return (z * self.X + x) * self.C + y * self.K + k

    def move(self, value, dz=0, dx=0, dy=0, dk=0):
        pairs = [
            (self.index(z, x, y, k), self.index(z ^ dz, x ^ dx, y ^ dy, k ^ dk))
            for z, x, y, k in self.devices()
        ]
        return lax.ppermute(value, ("row", "col"), pairs)

    def swap_xy(self, value):
        groups = [
            [self.index(z, x, y, k) for x in range(self.X) for y in range(self.Y)]
            for z in range(self.Z)
            for k in range(self.K)
        ]
        return lax.all_to_all(value, ("row", "col"), 0, 0, axis_index_groups=groups, tiled=True)

    def here(self):
        r, c = lax.axis_index("row"), lax.axis_index("col")
        return r // 2, r % 2, c // 2, c % 2


def params(**more):
    return pltpu.CompilerParams(vmem_limit_bytes=VMEM_LIMIT, **more)


def add_tiles(g, out, held, listed, slots, block, place):
    block_rows, block_cols, count = listed

    def one(s):
        wanted, row, col, turned = place(block_rows(s), block_cols(s))

        @pl.when(jnp.logical_and(s < count(), wanted))
        def _():
            tile = held[s]
            if turned:
                tile = tile.astype(F32).T.astype(BF16)
            out[
                pl.ds(pl.multiple_of(row * block, block), block),
                pl.ds(pl.multiple_of(col * block, block), block),
            ] = tile

    if slots <= 16:
        for s in range(slots):
            one(s)
    else:
        pl.loop(0, slots)(one)


def reader(listed, slots, at=0):
    first = at * (2 * slots + 1)
    return (
        lambda s: listed[first + s],
        lambda s: listed[first + slots + s],
        lambda: listed[first + 2 * slots],
    )


def multiply(matrix, stacked, outs, block):
    width = stacked.shape[1]
    tile = 256 if width % 256 == 0 else width

    def one(j):
        cols = pl.ds(j * tile if isinstance(j, int) else pl.multiple_of(j * tile, tile), tile)
        total = jnp.dot(matrix[...], stacked[:, cols], preferred_element_type=F32)
        for i, out in enumerate(outs):
            out[:, cols] = total[i * block : (i + 1) * block].astype(BF16)

    if matrix.shape[0] * matrix.shape[1] <= 2**20:
        for j in range(width // tile):
            one(j)
    else:
        pl.loop(0, width // tile)(one)


def forward_kernel(g, slots, block, n_in, *refs):
    lists, tiles = refs[:2], refs[2:4]
    blocks, outs = refs[4 : 4 + n_in], refs[4 + n_in : 4 + n_in + g.Z]
    matrix, stacked = refs[4 + n_in + g.Z :]
    z, x, y, k = g.here()
    matrix[...] = jnp.zeros_like(matrix)
    for dx in range(g.X):

        def place(row, col, dx=dx):
            at_z, at_x = row // g.X, row % g.X
            at_y, at_k = col // g.K, col % g.K
            at = dx * g.C + (at_y ^ y) * g.K + (at_k ^ k)
            return at_x == x, at_z ^ z, at, False

        add_tiles(g, matrix, tiles[dx], reader(lists[dx], slots), slots, block, place)
    for i, held in enumerate(blocks):
        stacked[pl.ds(i * block, block), :] = held[...]
    multiply(matrix, stacked, outs, block)


def forward(g, lists, tiles, blocks):
    slots = tiles[0].shape[0]
    block, width = blocks[0].shape
    n = len(blocks)
    return pl.pallas_call(
        functools.partial(forward_kernel, g, slots, block, n),
        out_shape=[jax.ShapeDtypeStruct((block, width), BF16)] * g.Z,
        in_specs=[SMEM_SPEC] * 2 + [VMEM_SPEC] * (2 + n),
        out_specs=[VMEM_SPEC] * g.Z,
        scratch_shapes=[
            pltpu.VMEM((g.Z * block, n * block), BF16),
            pltpu.VMEM((n * block, width), BF16),
        ],
        compiler_params=params(),
        cost_estimate=cost("forward"),
        name="forward",
    )(*lists, *tiles, *blocks)


def build_kernel(g, slots, block, *refs):
    lists, tiles, matrix = refs[:3], refs[3:7], refs[7]
    z, x, y, k = g.here()
    matrix[...] = jnp.zeros_like(matrix)
    for dk in range(g.K):
        for dx in range(g.X):

            def place(row, col, dk=dk, dx=dx):
                at_z, at_x = row // g.X, row % g.X
                at_y, at_k = col // g.K, col % g.K
                wanted = jnp.logical_and(at_x == x, at_k == k)
                return wanted, (x ^ dx) * g.Y + at_y, dk * g.Z + (at_z ^ z), True

            listed = reader(lists[2], slots, dx) if dk else reader(lists[dx], slots)
            add_tiles(g, matrix, tiles[dk * g.X + dx], listed, slots, block, place)


def build(g, lists, tiles):
    slots, block = tiles[0].shape[0], tiles[0].shape[1]
    return pl.pallas_call(
        functools.partial(build_kernel, g, slots, block),
        out_shape=jax.ShapeDtypeStruct((g.X * g.Y * block, g.K * g.Z * block), BF16),
        in_specs=[SMEM_SPEC] * 3 + [VMEM_SPEC] * 4,
        out_specs=VMEM_SPEC,
        compiler_params=params(),
        cost_estimate=cost("build"),
        name="build",
    )(*lists, *tiles)


def backward_kernel(g, block, groups, matrix, *refs):
    n_in = sum(groups)
    out, stacked = refs[n_in:]
    outs = [out.at[pl.ds(i * block, block)] for i in range(matrix.shape[0] // block)]
    at = 0
    for i, n in enumerate(groups):
        held = refs[at][...]
        for more in refs[at + 1 : at + n]:
            held = held + more[...]
        stacked[pl.ds(i * block, block), :] = held
        at += n
    multiply(matrix, stacked, outs, block)


def backward(g, matrix, groups):
    block, width = groups[0][0].shape
    flat = [v for group in groups for v in group]
    return pl.pallas_call(
        functools.partial(backward_kernel, g, block, [len(group) for group in groups]),
        out_shape=jax.ShapeDtypeStruct((matrix.shape[0], width), BF16),
        in_specs=[VMEM_SPEC] * (1 + len(flat)),
        out_specs=VMEM_SPEC,
        scratch_shapes=[pltpu.VMEM((len(groups) * block, width), BF16)],
        compiler_params=params(),
        cost_estimate=cost("backward"),
        name="backward",
    )(matrix, *flat)


def fold(g, split):
    total = split[0].astype(F32)
    for i in range(1, g.X * g.Y):
        total += g.move(split[i], dx=i // g.Y, dy=i % g.Y).astype(F32)
    return total


def layer_kernel(g, n_in, *refs):
    parts = refs[:n_in]
    weight, cotangent = refs[n_in : n_in + 2]
    activated, share, back, keep = refs[n_in + 2 : n_in + 6]
    agg = refs[n_in + 6]
    half = keep.shape[1]
    summed = parts[0][...].astype(F32)
    for part in parts[1:]:
        summed += part[...].astype(F32)
    agg[...] = summed.astype(BF16)
    core = g.here()[3]
    keep[...] = agg[:, pl.ds(pl.multiple_of(core * half, half), half)]
    share[:, :half] = agg[:, pl.ds(pl.multiple_of((1 - core) * half, half), half)]
    width = weight.shape[1]
    tile = 256 if width % 256 == 0 else width
    for j in range(width // tile):
        cols = slice(j * tile, (j + 1) * tile)
        hidden = jnp.dot(agg[...], weight[:, cols], preferred_element_type=F32)
        sigmoid = jax.nn.sigmoid(hidden)
        activated[:, cols] = (hidden * sigmoid).astype(BF16)
        slope = sigmoid * (1.0 + hidden * (1.0 - sigmoid))
        grad = (cotangent[:, cols].astype(F32) * slope).astype(BF16)
        share[:, half + j * tile : half + (j + 1) * tile] = grad
    back[...] = lax.dot_general(
        share[:, half:], weight[...], (((1,), (1,)), ((), ())), preferred_element_type=F32
    ).astype(BF16)


def layer(g, parts, weight, cotangent):
    rows, depth = parts[0].shape
    width = weight.shape[1]
    return pl.pallas_call(
        functools.partial(layer_kernel, g, len(parts)),
        out_shape=[
            jax.ShapeDtypeStruct((rows, width), BF16),
            jax.ShapeDtypeStruct((rows, depth // 2 + width), BF16),
            jax.ShapeDtypeStruct((rows, depth), BF16),
            jax.ShapeDtypeStruct((rows, depth // 2), BF16),
        ],
        in_specs=[VMEM_SPEC] * (len(parts) + 2),
        out_specs=[VMEM_SPEC] * 4,
        scratch_shapes=[pltpu.VMEM((rows, depth), BF16)],
        compiler_params=params(),
        cost_estimate=cost("layer"),
        name="layer",
    )(*parts, weight, cotangent)


def terms_kernel(g, keep, share, share_got, *refs):
    outs, turned, grads = refs[:-2], refs[-2], refs[-1]
    nodes, half = keep.shape
    both = jnp.concatenate([keep[...].astype(F32), share_got[:, :half].astype(F32)], axis=0)
    turned[...] = both.T.astype(BF16)
    z, x, y, _ = g.here()
    rows, width = outs[0].shape[1:]
    for dz in range(g.Z):
        cols = pl.ds(pl.multiple_of(half + (z ^ dz) * width, width), width)
        grads[0:nodes, dz * width : (dz + 1) * width] = share[:, cols]
        grads[nodes:, dz * width : (dz + 1) * width] = share_got[:, cols]
    for dx in range(g.X):
        for dy in range(g.Y):
            at = (x ^ dx) * g.Y + (y ^ dy)
            mine = turned[pl.ds(pl.multiple_of(at * rows, rows), rows), :]
            total = jnp.dot(mine, grads[...], preferred_element_type=F32).astype(BF16)
            for dz in range(g.Z):
                outs[dx * g.Y + dy][dz] = total[:, dz * width : (dz + 1) * width]


def terms(g, keep, share, share_got):
    nodes, half = keep.shape
    width = share.shape[1] - half
    n_out = g.X * g.Y
    shapes = [jax.ShapeDtypeStruct((g.Z, half // n_out, width // g.Z), BF16)] * n_out
    return pl.pallas_call(
        functools.partial(terms_kernel, g),
        out_shape=shapes,
        in_specs=[VMEM_SPEC] * 3,
        out_specs=[VMEM_SPEC] * len(shapes),
        scratch_shapes=[
            pltpu.VMEM((half, 2 * nodes), BF16),
            pltpu.VMEM((2 * nodes, width), BF16),
        ],
        compiler_params=params(),
        cost_estimate=cost("terms"),
        name="terms",
    )(keep, share, share_got)


def join_kernel(g, places, *refs):
    n = len(places)
    pieces, out = refs[:n], refs[n]
    held, whole, in_sems, out_sems = refs[n + 1 :]
    some, rows, width = pieces[0].shape
    z, x, y, k = g.here()
    copies = [pltpu.make_async_copy(v, held.at[i], in_sems.at[i]) for i, v in enumerate(pieces)]
    for copy in copies:
        copy.start()
    sent = []
    for i, (dk, dx, dy) in enumerate(places):
        copies[i].wait()
        at = ((k ^ dk) * g.X + (x ^ dx)) * g.Y + (y ^ dy)
        at = pl.ds(pl.multiple_of(at * rows, rows), rows)
        for dz in range(some):
            cols = pl.ds(pl.multiple_of((z ^ dz) * width, width), width)
            whole[i, :, cols] = held[i, dz].astype(F32)
        copy = pltpu.make_async_copy(whole.at[i], out.at[at], out_sems.at[i])
        copy.start()
        sent.append(copy)
    for copy in sent:
        copy.wait()


def join(g, places, pieces, shape):
    n = len(pieces)
    some, rows, width = pieces[0].shape
    return pl.pallas_call(
        functools.partial(join_kernel, g, places),
        out_shape=jax.ShapeDtypeStruct(shape, F32),
        in_specs=[HBM_SPEC] * n,
        out_specs=HBM_SPEC,
        scratch_shapes=[
            pltpu.VMEM((n, some, rows, width), BF16),
            pltpu.VMEM((n, rows, some * width), F32),
            pltpu.SemaphoreType.DMA((n,)),
            pltpu.SemaphoreType.DMA((n,)),
        ],
        compiler_params=params(),
        cost_estimate=cost("join"),
        name="join",
    )(*pieces)


def on_device(g, features, weight, cotangent, tile_values, block_row, block_column, tile_count):
    pin = lax.optimization_barrier

    def after(value, *others):
        return pin((value, others))[0]

    squares = [(dx, dy) for dx in range(g.X) for dy in range(g.Y)]

    listed = jnp.concatenate([block_row[0, 0], block_column[0, 0], tile_count[0]])
    lists = [listed, g.move(listed, dx=1)]
    tiles = [tile_values[0, 0], g.move(after(tile_values[0, 0], listed), dx=1)]
    near = {(0, 0): features}
    for dx, dy in [(1, 0)] + [at for at in squares[1:] if at != (1, 0)]:
        if dx and dy:
            near[dx, dy] = g.move(after(near[1, 0], lists[1]), dy=dy)
        else:
            near[dx, dy] = g.move(after(features, listed), dx=dx, dy=dy)
    blocks = []
    for at in squares:
        value = near[at] if at != (0, 0) else after(features, near[1, 0])
        blocks += [near[at], g.move(value, dk=1)]
    others = [g.move(after(tiles[0], near[1, 0]), dk=1)]
    lists.append(g.move(jnp.concatenate(lists), dk=1))
    blocks[0] = after(blocks[0], (others, lists[2]))
    sums = forward(g, lists[:2], tiles, blocks)
    parts = [sums[0]] + [g.move(sums[dz], dz=dz) for dz in range(1, g.Z)]
    others.append(g.move(after(tiles[1], sums), dk=1))
    matrix = build(g, lists, tiles + others)
    parts, matrix = pin((parts, matrix))
    activated, share, back, keep = layer(g, parts, weight, cotangent)

    shares = terms(g, keep, share, g.move(share, dk=1))

    groups = [[back]] + [[g.move(back, dz=dz)] for dz in range(1, g.Z)]
    arrived = groups[1:]
    groups += [[g.move(v, dk=1) for v in group] for group in groups]
    deltas = backward(g, matrix, groups)
    feat = g.swap_xy(deltas).astype(F32).reshape(g.X * g.Y, -1, deltas.shape[1])
    feat_grad = jnp.sum(feat, axis=0).astype(BF16)

    pieces = after(fold(g, shares).astype(BF16), arrived)
    total = pieces[0].astype(F32)
    for dz in range(1, g.Z):
        total += g.move(pieces[dz], dz=dz).astype(F32)
    factor = (features.shape[0] * g.R * g.C) ** (-0.5)
    own = (total * factor).astype(BF16)
    column = jnp.stack([own] + [g.move(own, dz=dz) for dz in range(1, g.Z)])
    column = after(column, deltas)
    held = [column if at == (0, 0) else g.move(column, dx=at[0], dy=at[1]) for at in squares]
    held += [g.move(v, dk=1) for v in held]
    places = [(dk, *at) for dk in range(g.K) for at in squares]
    held[-1] = after(held[-1], feat_grad)
    weight_grad = join(g, places, held, weight.shape)
    return (activated, feat_grad, weight_grad)


def solution(mesh):
    g = Grid(mesh.shape["row"], mesh.shape["col"])
    return jax.shard_map(
        functools.partial(on_device, g),
        mesh=mesh,
        in_specs=(
            P(("row", "col"), None),
            P(),
            P(("col", "row"), None),
            P("row", "col", None, None, None),
            P("row", "col", None),
            P("row", "col", None),
            P("row", "col"),
        ),
        out_specs=(P(("col", "row"), None), P(("row", "col"), None), P()),
        check_vma=False,
    )
```

```python
import functools

import jax
import jax.numpy as jnp
from jax import lax
from jax.experimental import pallas as pl
from jax.experimental.pallas import tpu as pltpu
from jax.sharding import PartitionSpec as P

BF16 = jnp.bfloat16
F32 = jnp.float32
VMEM_LIMIT = 64 * 2**20 - 2**18
SMEM_SPEC = pl.BlockSpec(memory_space=pltpu.SMEM)
VMEM_SPEC = pl.BlockSpec(memory_space=pltpu.VMEM)
HBM_SPEC = pl.BlockSpec(memory_space=pl.ANY)


COST = {}


def cost(name):
    return pl.CostEstimate(flops=0, bytes_accessed=COST.get(name, 0), transcendentals=0)


class Grid:
    def __init__(self, rows, cols):
        if rows & (rows - 1) or cols & (cols - 1) or min(rows, cols) < 2:
            raise ValueError("mesh axes")
        self.R, self.C = rows, cols
        self.X, self.K = 2, 2
        self.Z, self.Y = rows // 2, cols // 2

    def devices(self):
        for z in range(self.Z):
            for x in range(self.X):
                for y in range(self.Y):
                    for k in range(self.K):
                        yield z, x, y, k

    def index(self, z, x, y, k):
        return (z * self.X + x) * self.C + y * self.K + k

    def move(self, value, dz=0, dx=0, dy=0, dk=0):
        pairs = [
            (self.index(z, x, y, k), self.index(z ^ dz, x ^ dx, y ^ dy, k ^ dk))
            for z, x, y, k in self.devices()
        ]
        return lax.ppermute(value, ("row", "col"), pairs)

    def swap_xy(self, value):
        groups = [
            [self.index(z, x, y, k) for x in range(self.X) for y in range(self.Y)]
            for z in range(self.Z)
            for k in range(self.K)
        ]
        return lax.all_to_all(value, ("row", "col"), 0, 0, axis_index_groups=groups, tiled=True)

    def here(self):
        r, c = lax.axis_index("row"), lax.axis_index("col")
        return r // 2, r % 2, c // 2, c % 2


def params(**more):
    return pltpu.CompilerParams(vmem_limit_bytes=VMEM_LIMIT, **more)


def add_tiles(g, out, held, listed, slots, block, place):
    block_rows, block_cols, count = listed

    def one(s):
        wanted, row, col, turned = place(block_rows(s), block_cols(s))

        @pl.when(jnp.logical_and(s < count(), wanted))
        def _():
            tile = held[s]
            if turned:
                tile = tile.astype(F32).T.astype(BF16)
            out[
                pl.ds(pl.multiple_of(row * block, block), block),
                pl.ds(pl.multiple_of(col * block, block), block),
            ] = tile

    if slots <= 16:
        for s in range(slots):
            one(s)
    else:
        pl.loop(0, slots)(one)


def reader(listed, slots, at=0):
    first = at * (2 * slots + 1)
    return (
        lambda s: listed[first + s],
        lambda s: listed[first + slots + s],
        lambda: listed[first + 2 * slots],
    )


def multiply(matrix, stacked, outs, block):
    width = stacked.shape[1]
    tile = 256 if width % 256 == 0 else width

    def one(j):
        cols = pl.ds(j * tile if isinstance(j, int) else pl.multiple_of(j * tile, tile), tile)
        total = jnp.dot(matrix[...], stacked[:, cols], preferred_element_type=F32)
        for i, out in enumerate(outs):
            out[:, cols] = total[i * block : (i + 1) * block].astype(BF16)

    if matrix.shape[0] * matrix.shape[1] <= 2**20:
        for j in range(width // tile):
            one(j)
    else:
        pl.loop(0, width // tile)(one)


def forward_kernel(g, slots, block, n_in, *refs):
    lists, tiles = refs[:2], refs[2:4]
    blocks, outs = refs[4 : 4 + n_in], refs[4 + n_in : 4 + n_in + g.Z]
    matrix, stacked = refs[4 + n_in + g.Z :]
    z, x, y, k = g.here()
    matrix[...] = jnp.zeros_like(matrix)
    for dx in range(g.X):

        def place(row, col, dx=dx):
            at_z, at_x = row // g.X, row % g.X
            at_y, at_k = col // g.K, col % g.K
            at = dx * g.C + (at_y ^ y) * g.K + (at_k ^ k)
            return at_x == x, at_z ^ z, at, False

        add_tiles(g, matrix, tiles[dx], reader(lists[dx], slots), slots, block, place)
    for i, held in enumerate(blocks):
        stacked[pl.ds(i * block, block), :] = held[...]
    multiply(matrix, stacked, outs, block)


def forward(g, lists, tiles, blocks):
    slots = tiles[0].shape[0]
    block, width = blocks[0].shape
    n = len(blocks)
    return pl.pallas_call(
        functools.partial(forward_kernel, g, slots, block, n),
        out_shape=[jax.ShapeDtypeStruct((block, width), BF16)] * g.Z,
        in_specs=[SMEM_SPEC] * 2 + [VMEM_SPEC] * (2 + n),
        out_specs=[VMEM_SPEC] * g.Z,
        scratch_shapes=[
            pltpu.VMEM((g.Z * block, n * block), BF16),
            pltpu.VMEM((n * block, width), BF16),
        ],
        compiler_params=params(),
        cost_estimate=cost("forward"),
        name="forward",
    )(*lists, *tiles, *blocks)


def build_kernel(g, slots, block, *refs):
    lists, tiles, matrix = refs[:3], refs[3:7], refs[7]
    z, x, y, k = g.here()
    matrix[...] = jnp.zeros_like(matrix)
    for dk in range(g.K):
        for dx in range(g.X):

            def place(row, col, dk=dk, dx=dx):
                at_z, at_x = row // g.X, row % g.X
                at_y, at_k = col // g.K, col % g.K
                wanted = jnp.logical_and(at_x == x, at_k == k)
                return wanted, (x ^ dx) * g.Y + at_y, dk * g.Z + (at_z ^ z), True

            listed = reader(lists[2], slots, dx) if dk else reader(lists[dx], slots)
            add_tiles(g, matrix, tiles[dk * g.X + dx], listed, slots, block, place)


def build(g, lists, tiles):
    slots, block = tiles[0].shape[0], tiles[0].shape[1]
    return pl.pallas_call(
        functools.partial(build_kernel, g, slots, block),
        out_shape=jax.ShapeDtypeStruct((g.X * g.Y * block, g.K * g.Z * block), BF16),
        in_specs=[SMEM_SPEC] * 3 + [VMEM_SPEC] * 4,
        out_specs=VMEM_SPEC,
        compiler_params=params(),
        cost_estimate=cost("build"),
        name="build",
    )(*lists, *tiles)


def backward_kernel(g, block, groups, matrix, *refs):
    n_in = sum(groups)
    out, stacked = refs[n_in:]
    outs = [out.at[pl.ds(i * block, block)] for i in range(matrix.shape[0] // block)]
    at = 0
    for i, n in enumerate(groups):
        held = refs[at][...]
        for more in refs[at + 1 : at + n]:
            held = held + more[...]
        stacked[pl.ds(i * block, block), :] = held
        at += n
    multiply(matrix, stacked, outs, block)


def backward(g, matrix, groups):
    block, width = groups[0][0].shape
    flat = [v for group in groups for v in group]
    return pl.pallas_call(
        functools.partial(backward_kernel, g, block, [len(group) for group in groups]),
        out_shape=jax.ShapeDtypeStruct((matrix.shape[0], width), BF16),
        in_specs=[VMEM_SPEC] * (1 + len(flat)),
        out_specs=VMEM_SPEC,
        scratch_shapes=[pltpu.VMEM((len(groups) * block, width), BF16)],
        compiler_params=params(),
        cost_estimate=cost("backward"),
        name="backward",
    )(matrix, *flat)


def fold(g, split):
    total = split[0].astype(F32)
    for i in range(1, g.X * g.Y):
        total += g.move(split[i], dx=i // g.Y, dy=i % g.Y).astype(F32)
    return total


def layer_kernel(g, n_in, *refs):
    parts = refs[:n_in]
    weight, cotangent = refs[n_in : n_in + 2]
    activated, share, back, keep = refs[n_in + 2 : n_in + 6]
    agg = refs[n_in + 6]
    half = keep.shape[1]
    summed = parts[0][...].astype(F32)
    for part in parts[1:]:
        summed += part[...].astype(F32)
    agg[...] = summed.astype(BF16)
    core = g.here()[3]
    keep[...] = agg[:, pl.ds(pl.multiple_of(core * half, half), half)]
    share[:, :half] = agg[:, pl.ds(pl.multiple_of((1 - core) * half, half), half)]
    width = weight.shape[1]
    tile = 256 if width % 256 == 0 else width
    for j in range(width // tile):
        cols = slice(j * tile, (j + 1) * tile)
        hidden = jnp.dot(agg[...], weight[:, cols], preferred_element_type=F32)
        sigmoid = jax.nn.sigmoid(hidden)
        activated[:, cols] = (hidden * sigmoid).astype(BF16)
        slope = sigmoid * (1.0 + hidden * (1.0 - sigmoid))
        grad = (cotangent[:, cols].astype(F32) * slope).astype(BF16)
        share[:, half + j * tile : half + (j + 1) * tile] = grad
    back[...] = lax.dot_general(
        share[:, half:], weight[...], (((1,), (1,)), ((), ())), preferred_element_type=F32
    ).astype(BF16)


def layer(g, parts, weight, cotangent):
    rows, depth = parts[0].shape
    width = weight.shape[1]
    return pl.pallas_call(
        functools.partial(layer_kernel, g, len(parts)),
        out_shape=[
            jax.ShapeDtypeStruct((rows, width), BF16),
            jax.ShapeDtypeStruct((rows, depth // 2 + width), BF16),
            jax.ShapeDtypeStruct((rows, depth), BF16),
            jax.ShapeDtypeStruct((rows, depth // 2), BF16),
        ],
        in_specs=[VMEM_SPEC] * (len(parts) + 2),
        out_specs=[VMEM_SPEC] * 4,
        scratch_shapes=[pltpu.VMEM((rows, depth), BF16)],
        compiler_params=params(),
        cost_estimate=cost("layer"),
        name="layer",
    )(*parts, weight, cotangent)


def terms_kernel(g, keep, share, share_got, *refs):
    outs, turned, grads = refs[:-2], refs[-2], refs[-1]
    nodes, half = keep.shape
    both = jnp.concatenate([keep[...].astype(F32), share_got[:, :half].astype(F32)], axis=0)
    turned[...] = both.T.astype(BF16)
    z, x, y, _ = g.here()
    rows, width = outs[0].shape[1:]
    for dz in range(g.Z):
        cols = pl.ds(pl.multiple_of(half + (z ^ dz) * width, width), width)
        grads[0:nodes, dz * width : (dz + 1) * width] = share[:, cols]
        grads[nodes:, dz * width : (dz + 1) * width] = share_got[:, cols]
    for dx in range(g.X):
        for dy in range(g.Y):
            at = (x ^ dx) * g.Y + (y ^ dy)
            mine = turned[pl.ds(pl.multiple_of(at * rows, rows), rows), :]
            total = jnp.dot(mine, grads[...], preferred_element_type=F32).astype(BF16)
            for dz in range(g.Z):
                outs[dx * g.Y + dy][dz] = total[:, dz * width : (dz + 1) * width]


def terms(g, keep, share, share_got):
    nodes, half = keep.shape
    width = share.shape[1] - half
    n_out = g.X * g.Y
    shapes = [jax.ShapeDtypeStruct((g.Z, half // n_out, width // g.Z), BF16)] * n_out
    return pl.pallas_call(
        functools.partial(terms_kernel, g),
        out_shape=shapes,
        in_specs=[VMEM_SPEC] * 3,
        out_specs=[VMEM_SPEC] * len(shapes),
        scratch_shapes=[
            pltpu.VMEM((half, 2 * nodes), BF16),
            pltpu.VMEM((2 * nodes, width), BF16),
        ],
        compiler_params=params(),
        cost_estimate=cost("terms"),
        name="terms",
    )(keep, share, share_got)


def join_kernel(g, places, *refs):
    n = len(places)
    pieces, out = refs[:n], refs[n]
    held, whole, in_sems, out_sems = refs[n + 1 :]
    some, rows, width = pieces[0].shape
    z, x, y, k = g.here()
    copies = [pltpu.make_async_copy(v, held.at[i], in_sems.at[i]) for i, v in enumerate(pieces)]
    for copy in copies:
        copy.start()
    sent = []
    for i, (dk, dx, dy) in enumerate(places):
        copies[i].wait()
        at = ((k ^ dk) * g.X + (x ^ dx)) * g.Y + (y ^ dy)
        at = pl.ds(pl.multiple_of(at * rows, rows), rows)
        for dz in range(some):
            cols = pl.ds(pl.multiple_of((z ^ dz) * width, width), width)
            whole[i, :, cols] = held[i, dz].astype(F32)
        copy = pltpu.make_async_copy(whole.at[i], out.at[at], out_sems.at[i])
        copy.start()
        sent.append(copy)
    for copy in sent:
        copy.wait()


def join(g, places, pieces, shape):
    n = len(pieces)
    some, rows, width = pieces[0].shape
    return pl.pallas_call(
        functools.partial(join_kernel, g, places),
        out_shape=jax.ShapeDtypeStruct(shape, F32),
        in_specs=[HBM_SPEC] * n,
        out_specs=HBM_SPEC,
        scratch_shapes=[
            pltpu.VMEM((n, some, rows, width), BF16),
            pltpu.VMEM((n, rows, some * width), F32),
            pltpu.SemaphoreType.DMA((n,)),
            pltpu.SemaphoreType.DMA((n,)),
        ],
        compiler_params=params(),
        cost_estimate=cost("join"),
        name="join",
    )(*pieces)


def on_device(g, features, weight, cotangent, tile_values, block_row, block_column, tile_count):
    pin = lax.optimization_barrier

    def after(value, *others):
        return pin((value, others))[0]

    squares = [(dx, dy) for dx in range(g.X) for dy in range(g.Y)]

    listed = jnp.concatenate([block_row[0, 0], block_column[0, 0], tile_count[0]])
    lists = [listed, g.move(listed, dx=1)]
    tiles = [tile_values[0, 0], g.move(after(tile_values[0, 0], listed), dx=1)]
    near = {(0, 0): features}
    for dx, dy in [(1, 0)] + [at for at in squares[1:] if at != (1, 0)]:
        if dx and dy:
            near[dx, dy] = g.move(after(near[1, 0], lists[1]), dy=dy)
        else:
            near[dx, dy] = g.move(after(features, listed), dx=dx, dy=dy)
    blocks = []
    for at in squares:
        value = near[at] if at != (0, 0) else after(features, near[1, 0])
        blocks += [near[at], g.move(value, dk=1)]
    others = [g.move(after(tiles[0], near[1, 0]), dk=1)]
    lists.append(g.move(jnp.concatenate(lists), dk=1))
    blocks[0] = after(blocks[0], (others, lists[2]))
    sums = forward(g, lists[:2], tiles, blocks)
    parts = [sums[0]] + [g.move(sums[dz], dz=dz) for dz in range(1, g.Z)]
    others.append(g.move(after(tiles[1], sums), dk=1))
    matrix = build(g, lists, tiles + others)
    parts, matrix = pin((parts, matrix))
    activated, share, back, keep = layer(g, parts, weight, cotangent)

    shares = terms(g, keep, share, g.move(share, dk=1))

    groups = [[back]] + [[g.move(back, dz=dz)] for dz in range(1, g.Z)]
    arrived = groups[1:]
    groups += [[g.move(v, dk=1) for v in group] for group in groups]
    deltas = backward(g, matrix, groups)
    feat = g.swap_xy(deltas).astype(F32).reshape(g.X * g.Y, -1, deltas.shape[1])
    feat_grad = jnp.sum(feat, axis=0).astype(BF16)

    moved = [shares[0]]
    moved += [g.move(v, dx=at[0], dy=at[1]) for at, v in list(zip(squares, shares))[1:]]
    moved = after(moved, arrived)
    pieces = [sum(v[dz].astype(F32) for v in moved) for dz in range(g.Z)]
    total = pieces[0]
    pieces = [v.astype(BF16) for v in pieces]
    for dz in range(1, g.Z):
        total += g.move(pieces[dz], dz=dz).astype(F32)
    factor = (features.shape[0] * g.R * g.C) ** (-0.5)
    own = (total * factor).astype(BF16)
    column = jnp.stack([own] + [g.move(own, dz=dz) for dz in range(1, g.Z)])
    column = after(column, deltas)
    held = [column if at == (0, 0) else g.move(column, dx=at[0], dy=at[1]) for at in squares]
    held += [g.move(v, dk=1) for v in held]
    places = [(dk, *at) for dk in range(g.K) for at in squares]
    held[-1] = after(held[-1], feat_grad)
    weight_grad = join(g, places, held, weight.shape)
    return (activated, feat_grad, weight_grad)


def solution(mesh):
    g = Grid(mesh.shape["row"], mesh.shape["col"])
    return jax.shard_map(
        functools.partial(on_device, g),
        mesh=mesh,
        in_specs=(
            P(("row", "col"), None),
            P(),
            P(("col", "row"), None),
            P("row", "col", None, None, None),
            P("row", "col", None),
            P("row", "col", None),
            P("row", "col"),
        ),
        out_specs=(P(("col", "row"), None), P(("row", "col"), None), P()),
        check_vma=False,
    )
```

```python
import functools

import jax
import jax.numpy as jnp
from jax import lax
from jax.experimental import pallas as pl
from jax.experimental.pallas import tpu as pltpu
from jax.sharding import PartitionSpec as P

BF16 = jnp.bfloat16
F32 = jnp.float32
VMEM_LIMIT = 64 * 2**20 - 2**18
SMEM_SPEC = pl.BlockSpec(memory_space=pltpu.SMEM)
VMEM_SPEC = pl.BlockSpec(memory_space=pltpu.VMEM)
HBM_SPEC = pl.BlockSpec(memory_space=pl.ANY)


COST = {}


def cost(name):
    return pl.CostEstimate(flops=0, bytes_accessed=COST.get(name, 0), transcendentals=0)


class Grid:
    def __init__(self, rows, cols):
        if rows & (rows - 1) or cols & (cols - 1) or min(rows, cols) < 2:
            raise ValueError("mesh axes")
        self.R, self.C = rows, cols
        self.X, self.K = 2, 2
        self.Z, self.Y = rows // 2, cols // 2

    def devices(self):
        for z in range(self.Z):
            for x in range(self.X):
                for y in range(self.Y):
                    for k in range(self.K):
                        yield z, x, y, k

    def index(self, z, x, y, k):
        return (z * self.X + x) * self.C + y * self.K + k

    def move(self, value, dz=0, dx=0, dy=0, dk=0):
        pairs = [
            (self.index(z, x, y, k), self.index(z ^ dz, x ^ dx, y ^ dy, k ^ dk))
            for z, x, y, k in self.devices()
        ]
        return lax.ppermute(value, ("row", "col"), pairs)

    def swap_xy(self, value):
        groups = [
            [self.index(z, x, y, k) for x in range(self.X) for y in range(self.Y)]
            for z in range(self.Z)
            for k in range(self.K)
        ]
        return lax.all_to_all(value, ("row", "col"), 0, 0, axis_index_groups=groups, tiled=True)

    def here(self):
        r, c = lax.axis_index("row"), lax.axis_index("col")
        return r // 2, r % 2, c // 2, c % 2


def params(**more):
    return pltpu.CompilerParams(vmem_limit_bytes=VMEM_LIMIT, **more)


def add_tiles(g, out, held, listed, slots, block, place):
    block_rows, block_cols, count = listed

    def one(s):
        wanted, row, col, turned = place(block_rows(s), block_cols(s))

        @pl.when(jnp.logical_and(s < count(), wanted))
        def _():
            tile = held[s]
            if turned:
                tile = tile.astype(F32).T.astype(BF16)
            out[
                pl.ds(pl.multiple_of(row * block, block), block),
                pl.ds(pl.multiple_of(col * block, block), block),
            ] = tile

    if slots <= 16:
        for s in range(slots):
            one(s)
    else:
        pl.loop(0, slots)(one)


def reader(listed, slots, at=0):
    first = at * (2 * slots + 1)
    return (
        lambda s: listed[first + s],
        lambda s: listed[first + slots + s],
        lambda: listed[first + 2 * slots],
    )


def multiply(matrix, stacked, outs, block):
    width = stacked.shape[1]
    tile = 256 if width % 256 == 0 else width

    def one(j):
        cols = pl.ds(j * tile if isinstance(j, int) else pl.multiple_of(j * tile, tile), tile)
        total = jnp.dot(matrix[...], stacked[:, cols], preferred_element_type=F32)
        for i, out in enumerate(outs):
            out[:, cols] = total[i * block : (i + 1) * block].astype(BF16)

    if matrix.shape[0] * matrix.shape[1] <= 2**20:
        for j in range(width // tile):
            one(j)
    else:
        pl.loop(0, width // tile)(one)


def forward_kernel(g, slots, block, n_in, *refs):
    lists, tiles = refs[:2], refs[2:4]
    blocks, outs = refs[4 : 4 + n_in], refs[4 + n_in : 4 + n_in + g.Z]
    matrix, stacked = refs[4 + n_in + g.Z :]
    z, x, y, k = g.here()
    matrix[...] = jnp.zeros_like(matrix)
    for dx in range(g.X):

        def place(row, col, dx=dx):
            at_z, at_x = row // g.X, row % g.X
            at_y, at_k = col // g.K, col % g.K
            at = dx * g.C + (at_y ^ y) * g.K + (at_k ^ k)
            return at_x == x, at_z ^ z, at, False

        add_tiles(g, matrix, tiles[dx], reader(lists[dx], slots), slots, block, place)
    for i, held in enumerate(blocks):
        stacked[pl.ds(i * block, block), :] = held[...]
    multiply(matrix, stacked, outs, block)


def forward(g, lists, tiles, blocks):
    slots = tiles[0].shape[0]
    block, width = blocks[0].shape
    n = len(blocks)
    return pl.pallas_call(
        functools.partial(forward_kernel, g, slots, block, n),
        out_shape=[jax.ShapeDtypeStruct((block, width), BF16)] * g.Z,
        in_specs=[SMEM_SPEC] * 2 + [VMEM_SPEC] * (2 + n),
        out_specs=[VMEM_SPEC] * g.Z,
        scratch_shapes=[
            pltpu.VMEM((g.Z * block, n * block), BF16),
            pltpu.VMEM((n * block, width), BF16),
        ],
        compiler_params=params(),
        cost_estimate=cost("forward"),
        name="forward",
    )(*lists, *tiles, *blocks)


def build_kernel(g, slots, block, *refs):
    lists, tiles, matrix = refs[:3], refs[3:7], refs[7]
    z, x, y, k = g.here()
    matrix[...] = jnp.zeros_like(matrix)
    for dk in range(g.K):
        for dx in range(g.X):

            def place(row, col, dk=dk, dx=dx):
                at_z, at_x = row // g.X, row % g.X
                at_y, at_k = col // g.K, col % g.K
                wanted = jnp.logical_and(at_x == x, at_k == k)
                return wanted, (x ^ dx) * g.Y + at_y, dk * g.Z + (at_z ^ z), True

            listed = reader(lists[2], slots, dx) if dk else reader(lists[dx], slots)
            add_tiles(g, matrix, tiles[dk * g.X + dx], listed, slots, block, place)


def build(g, lists, tiles):
    slots, block = tiles[0].shape[0], tiles[0].shape[1]
    return pl.pallas_call(
        functools.partial(build_kernel, g, slots, block),
        out_shape=jax.ShapeDtypeStruct((g.X * g.Y * block, g.K * g.Z * block), BF16),
        in_specs=[SMEM_SPEC] * 3 + [VMEM_SPEC] * 4,
        out_specs=VMEM_SPEC,
        compiler_params=params(),
        cost_estimate=cost("build"),
        name="build",
    )(*lists, *tiles)


def backward_kernel(g, block, groups, matrix, *refs):
    n_in = sum(groups)
    out, stacked = refs[n_in:]
    outs = [out.at[pl.ds(i * block, block)] for i in range(matrix.shape[0] // block)]
    at = 0
    for i, n in enumerate(groups):
        held = refs[at][...]
        for more in refs[at + 1 : at + n]:
            held = held + more[...]
        stacked[pl.ds(i * block, block), :] = held
        at += n
    multiply(matrix, stacked, outs, block)


def backward(g, matrix, groups):
    block, width = groups[0][0].shape
    flat = [v for group in groups for v in group]
    return pl.pallas_call(
        functools.partial(backward_kernel, g, block, [len(group) for group in groups]),
        out_shape=jax.ShapeDtypeStruct((matrix.shape[0], width), BF16),
        in_specs=[VMEM_SPEC] * (1 + len(flat)),
        out_specs=VMEM_SPEC,
        scratch_shapes=[pltpu.VMEM((len(groups) * block, width), BF16)],
        compiler_params=params(),
        cost_estimate=cost("backward"),
        name="backward",
    )(matrix, *flat)


def fold(g, split):
    total = split[0].astype(F32)
    for i in range(1, g.X * g.Y):
        total += g.move(split[i], dx=i // g.Y, dy=i % g.Y).astype(F32)
    return total


def layer_kernel(g, n_in, *refs):
    parts = refs[:n_in]
    weight, cotangent = refs[n_in : n_in + 2]
    activated, share, back, keep = refs[n_in + 2 : n_in + 6]
    agg = refs[n_in + 6]
    half = keep.shape[1]
    summed = parts[0][...].astype(F32)
    for part in parts[1:]:
        summed += part[...].astype(F32)
    agg[...] = summed.astype(BF16)
    core = g.here()[3]
    keep[...] = agg[:, pl.ds(pl.multiple_of(core * half, half), half)]
    share[:, :half] = agg[:, pl.ds(pl.multiple_of((1 - core) * half, half), half)]
    width = weight.shape[1]
    tile = 256 if width % 256 == 0 else width
    for j in range(width // tile):
        cols = slice(j * tile, (j + 1) * tile)
        hidden = jnp.dot(agg[...], weight[:, cols], preferred_element_type=F32)
        sigmoid = jax.nn.sigmoid(hidden)
        activated[:, cols] = (hidden * sigmoid).astype(BF16)
        slope = sigmoid * (1.0 + hidden * (1.0 - sigmoid))
        grad = (cotangent[:, cols].astype(F32) * slope).astype(BF16)
        share[:, half + j * tile : half + (j + 1) * tile] = grad
    back[...] = lax.dot_general(
        share[:, half:], weight[...], (((1,), (1,)), ((), ())), preferred_element_type=F32
    ).astype(BF16)


def layer(g, parts, weight, cotangent):
    rows, depth = parts[0].shape
    width = weight.shape[1]
    return pl.pallas_call(
        functools.partial(layer_kernel, g, len(parts)),
        out_shape=[
            jax.ShapeDtypeStruct((rows, width), BF16),
            jax.ShapeDtypeStruct((rows, depth // 2 + width), BF16),
            jax.ShapeDtypeStruct((rows, depth), BF16),
            jax.ShapeDtypeStruct((rows, depth // 2), BF16),
        ],
        in_specs=[VMEM_SPEC] * (len(parts) + 2),
        out_specs=[VMEM_SPEC] * 4,
        scratch_shapes=[pltpu.VMEM((rows, depth), BF16)],
        compiler_params=params(),
        cost_estimate=cost("layer"),
        name="layer",
    )(*parts, weight, cotangent)


def terms_kernel(g, keep, share, share_got, *refs):
    outs, turned, grads = refs[:-2], refs[-2], refs[-1]
    nodes, half = keep.shape
    turned[:, :nodes] = keep[...].T
    turned[:, nodes:] = share_got[:, :half].T
    z, x, y, _ = g.here()
    rows, width = outs[0].shape[1:]
    for dz in range(g.Z):
        cols = pl.ds(pl.multiple_of(half + (z ^ dz) * width, width), width)
        grads[0:nodes, dz * width : (dz + 1) * width] = share[:, cols]
        grads[nodes:, dz * width : (dz + 1) * width] = share_got[:, cols]
    for dx in range(g.X):
        for dy in range(g.Y):
            at = (x ^ dx) * g.Y + (y ^ dy)
            mine = turned[pl.ds(pl.multiple_of(at * rows, rows), rows), :]
            total = jnp.dot(mine, grads[...], preferred_element_type=F32).astype(BF16)
            for dz in range(g.Z):
                outs[dx * g.Y + dy][dz] = total[:, dz * width : (dz + 1) * width]


def terms(g, keep, share, share_got):
    nodes, half = keep.shape
    width = share.shape[1] - half
    n_out = g.X * g.Y
    shapes = [jax.ShapeDtypeStruct((g.Z, half // n_out, width // g.Z), BF16)] * n_out
    return pl.pallas_call(
        functools.partial(terms_kernel, g),
        out_shape=shapes,
        in_specs=[VMEM_SPEC] * 3,
        out_specs=[VMEM_SPEC] * len(shapes),
        scratch_shapes=[
            pltpu.VMEM((half, 2 * nodes), BF16),
            pltpu.VMEM((2 * nodes, width), BF16),
        ],
        compiler_params=params(),
        cost_estimate=cost("terms"),
        name="terms",
    )(keep, share, share_got)


def join_kernel(g, places, *refs):
    n = len(places)
    pieces, out = refs[:n], refs[n]
    held, whole, in_sems, out_sems = refs[n + 1 :]
    some, rows, width = pieces[0].shape
    z, x, y, k = g.here()
    copies = [pltpu.make_async_copy(v, held.at[i], in_sems.at[i]) for i, v in enumerate(pieces)]
    for copy in copies:
        copy.start()
    sent = []
    for i, (dk, dx, dy) in enumerate(places):
        copies[i].wait()
        at = ((k ^ dk) * g.X + (x ^ dx)) * g.Y + (y ^ dy)
        at = pl.ds(pl.multiple_of(at * rows, rows), rows)
        for dz in range(some):
            cols = pl.ds(pl.multiple_of((z ^ dz) * width, width), width)
            whole[i, :, cols] = held[i, dz].astype(F32)
        copy = pltpu.make_async_copy(whole.at[i], out.at[at], out_sems.at[i])
        copy.start()
        sent.append(copy)
    for copy in sent:
        copy.wait()


def join(g, places, pieces, shape):
    n = len(pieces)
    some, rows, width = pieces[0].shape
    return pl.pallas_call(
        functools.partial(join_kernel, g, places),
        out_shape=jax.ShapeDtypeStruct(shape, F32),
        in_specs=[HBM_SPEC] * n,
        out_specs=HBM_SPEC,
        scratch_shapes=[
            pltpu.VMEM((n, some, rows, width), BF16),
            pltpu.VMEM((n, rows, some * width), F32),
            pltpu.SemaphoreType.DMA((n,)),
            pltpu.SemaphoreType.DMA((n,)),
        ],
        compiler_params=params(),
        cost_estimate=cost("join"),
        name="join",
    )(*pieces)


def on_device(g, features, weight, cotangent, tile_values, block_row, block_column, tile_count):
    pin = lax.optimization_barrier

    def after(value, *others):
        return pin((value, others))[0]

    squares = [(dx, dy) for dx in range(g.X) for dy in range(g.Y)]

    listed = jnp.concatenate([block_row[0, 0], block_column[0, 0], tile_count[0]])
    lists = [listed, g.move(listed, dx=1)]
    tiles = [tile_values[0, 0], g.move(after(tile_values[0, 0], listed), dx=1)]
    near = {(0, 0): features}
    for dx, dy in [(1, 0)] + [at for at in squares[1:] if at != (1, 0)]:
        if dx and dy:
            near[dx, dy] = g.move(after(near[1, 0], lists[1]), dy=dy)
        else:
            near[dx, dy] = g.move(after(features, listed), dx=dx, dy=dy)
    blocks = []
    for at in squares:
        value = near[at] if at != (0, 0) else after(features, near[1, 0])
        blocks += [near[at], g.move(value, dk=1)]
    others = [g.move(after(tiles[0], near[1, 0]), dk=1)]
    lists.append(g.move(jnp.concatenate(lists), dk=1))
    blocks[0] = after(blocks[0], (others, lists[2]))
    sums = forward(g, lists[:2], tiles, blocks)
    parts = [sums[0]] + [g.move(sums[dz], dz=dz) for dz in range(1, g.Z)]
    others.append(g.move(after(tiles[1], sums), dk=1))
    matrix = build(g, lists, tiles + others)
    parts, matrix = pin((parts, matrix))
    activated, share, back, keep = layer(g, parts, weight, cotangent)

    shares = terms(g, keep, share, g.move(share, dk=1))

    groups = [[back]] + [[g.move(back, dz=dz)] for dz in range(1, g.Z)]
    arrived = groups[1:]
    groups += [[g.move(v, dk=1) for v in group] for group in groups]
    deltas = backward(g, matrix, groups)
    feat = g.swap_xy(deltas).astype(F32).reshape(g.X * g.Y, -1, deltas.shape[1])
    feat_grad = jnp.sum(feat, axis=0).astype(BF16)

    moved = [shares[0]]
    moved += [g.move(v, dx=at[0], dy=at[1]) for at, v in list(zip(squares, shares))[1:]]
    moved = after(moved, arrived)
    pieces = [sum(v[dz].astype(F32) for v in moved) for dz in range(g.Z)]
    total = pieces[0]
    pieces = [v.astype(BF16) for v in pieces]
    for dz in range(1, g.Z):
        total += g.move(pieces[dz], dz=dz).astype(F32)
    factor = (features.shape[0] * g.R * g.C) ** (-0.5)
    own = (total * factor).astype(BF16)
    column = jnp.stack([own] + [g.move(own, dz=dz) for dz in range(1, g.Z)])
    column = after(column, deltas)
    held = [column if at == (0, 0) else g.move(column, dx=at[0], dy=at[1]) for at in squares]
    held += [g.move(v, dk=1) for v in held]
    places = [(dk, *at) for dk in range(g.K) for at in squares]
    held[-1] = after(held[-1], feat_grad)
    weight_grad = join(g, places, held, weight.shape)
    return (activated, feat_grad, weight_grad)


def solution(mesh):
    g = Grid(mesh.shape["row"], mesh.shape["col"])
    return jax.shard_map(
        functools.partial(on_device, g),
        mesh=mesh,
        in_specs=(
            P(("row", "col"), None),
            P(),
            P(("col", "row"), None),
            P("row", "col", None, None, None),
            P("row", "col", None),
            P("row", "col", None),
            P("row", "col"),
        ),
        out_specs=(P(("col", "row"), None), P(("row", "col"), None), P()),
        check_vma=False,
    )
```
